512 devices in a mesh: vol: 128 (over z, x, core), rep: 4 (over y).
Axes of the slice: x: 4, y: 4, z: 16, core: 2. Of those that a mesh axis runs over, the one named last changes fastest.
Arguments:
- cutouts: bfloat16 [4, 4096, 4096], P('rep', 'vol'), may hold values from -6 to 6
- counts: int32 [4, 128], P('rep', 'vol'), may hold values from 1 to 32, as said below
- partner: int32 [4, 2048], P('rep'), may hold values from 0 to 2047, as said below
- w_stem: bfloat16 [64, 128], replicated, may hold values from -0.75 to 0.75
- w_mix: bfloat16 [128, 128], replicated, may hold values from -0.5 to 0.5
- w_out: bfloat16 [128, 128], replicated, may hold values from -0.5 to 0.5
- w_proj: bfloat16 [128, 64], replicated, may hold values from -0.5 to 0.5
Outputs:
- upd_stem: float32 [64, 128], replicated
- upd_mix: float32 [128, 128], replicated
- upd_out: float32 [128, 128], replicated
- upd_proj: float32 [128, 64], replicated
- node_loss: float32 [4, 128, 16], P('rep', 'vol')
The draws below stay inside these ranges and needn't reach their ends.
Inputs may be any that keep to these rules, and one draw needn't show every extreme that they name: `counts`: each row sums to 2048, and its largest entry is exactly 32. Each row pairs the nodes of a group: partner[r, partner[r, g]] = g and partner[r, g] != g.
All inputs are finite; a program needn't handle non-finite values.
Results may differ from the reference program's by a relative error of at most 0.0035.
Values may be sent and summed in bfloat16 or wider, within the bound.
A program may use at most 64 MiB of HBM per device.

```python
import jax
import jax.numpy as jnp
from jax import lax

C = 128
E = 64
VOXP = 64
PATCH = 64
NODE_DEV = 16
MAXN = 32
NODES = 2048
N_VOL = 128
N_REP = 4


pattern_kinds = 12


def owner_counts(key):
    keys = jax.random.split(key, N_REP)

    def one_group(group_key):
        order_key, moves_key = jax.random.split(group_key)
        order = jax.random.permutation(order_key, N_VOL).astype(jnp.int32)
        moves = jax.random.randint(moves_key, (N_VOL,), 0, NODE_DEV, dtype=jnp.int32)
        position = jnp.arange(N_VOL, dtype=jnp.int32)
        beyond = position - 3
        pair_slot = jnp.clip(beyond // 2, 0, N_VOL - 1)
        amount = jnp.take(moves, pair_slot)
        mate = jnp.where(beyond % 2 == 0, position + 1, position - 1)
        paired = (beyond >= 0) & (mate < N_VOL)
        signed = jnp.where(beyond % 2 == 0, amount, -amount)
        values = NODE_DEV + jnp.where(paired, signed, 0)
        values = jnp.where(position == 0, MAXN, values)
        values = jnp.where(position == 1, 1, values)
        values = jnp.where(position == 2, NODE_DEV - 1, values)
        return jnp.zeros((N_VOL,), jnp.int32).at[order].set(values.astype(jnp.int32))
    return jax.vmap(one_group)(keys)


def draw_counts(key, part):
    return owner_counts(jax.random.fold_in(key, 29))


def draw_cutouts(key, part):
    group_counts = owner_counts(jax.random.fold_in(key, 29))
    offsets = (jnp.cumsum(group_counts, axis=1) - group_counts).astype(jnp.int32)
    slot = jnp.arange(MAXN, dtype=jnp.int32)
    node = (offsets[:, :, None] + slot[None, None, :]).reshape(N_REP, N_VOL * MAXN)
    kind = node % N_VOL % pattern_kinds
    pattern_key, single_key, noise_key = jax.random.split(jax.random.fold_in(key, 31), 3)
    patterns = 2.0 * jax.random.normal(pattern_key, (pattern_kinds, VOXP), jnp.float32)
    shared = jnp.take(patterns, kind, axis=0)
    single = jax.random.normal(single_key, (N_REP, N_VOL * MAXN, VOXP), jnp.float32)
    noise = jax.random.normal(noise_key, (N_REP, N_VOL * MAXN, PATCH, VOXP), jnp.float32)
    values = jnp.clip(shared[:, :, None, :] + single[:, :, None, :] + noise, -6.0, 6.0)
    return values.reshape(N_REP, N_VOL * MAXN, PATCH * VOXP).astype(jnp.bfloat16)


def draw_partner(key, part):
    keys = jax.random.split(jax.random.fold_in(key, 17), N_REP)

    def one_group(group_key):
        order = jax.random.permutation(group_key, NODES).astype(jnp.int32)
        pairs = order.reshape(NODES // 2, 2)
        paired = jnp.zeros((NODES,), jnp.int32)
        paired = paired.at[pairs[:, 0]].set(pairs[:, 1])
        paired = paired.at[pairs[:, 1]].set(pairs[:, 0])
        return paired
    return jax.vmap(one_group)(keys)


def centred(own_key, dims, spread, limit, kind=jnp.bfloat16):
    drawn = jax.random.normal(own_key, dims, jnp.float32) * spread
    return jnp.minimum(jnp.maximum(drawn, -limit), limit).astype(kind)


def setup_inputs(seed: int = 0) -> dict:
    arg_keys = jax.random.split(jax.random.key(seed), 8)
    cutouts = draw_cutouts(jax.random.fold_in(arg_keys[7], 71), 0)
    counts = draw_counts(jax.random.fold_in(arg_keys[7], 71), 0)
    partner = draw_partner(jax.random.fold_in(arg_keys[7], 71), 0)
    w_stem = centred(arg_keys[3], (VOXP, C), VOXP ** -0.5, 0.75)
    w_mix = centred(arg_keys[4], (C, C), C ** -0.5, 0.5)
    w_out = centred(arg_keys[5], (C, C), C ** -0.5, 0.5)
    w_proj = centred(arg_keys[6], (C, E), C ** -0.5, 0.5)
    return {"cutouts": cutouts, "counts": counts, "partner": partner, "w_stem": w_stem, "w_mix": w_mix, "w_out": w_out, "w_proj": w_proj}


logit_divisor_factor = 0.2
norm_eps = 1e-06
rms_eps = 1e-06

def first_dot(left, right):
    return lax.dot_general(left, right, (((0,), (0,)), ((), ())), preferred_element_type=jnp.float32)

def concluding_matrix_multiply(left, right):
    return lax.dot_general(left, right, (((1,), (1,)), ((), ())), preferred_element_type=jnp.float32)

def silu_slope(value):
    sigma = jax.nn.sigmoid(value)
    return sigma * (1.0 + value * (1.0 - sigma))

def encode(cutout_rows, w_stem, w_mix, w_out, w_proj):
    number = cutout_rows.shape[0]
    patches = cutout_rows.reshape(-1, w_stem.shape[0])
    per_cutout = patches.shape[0] // number
    pre_stem = jnp.dot(patches, w_stem, preferred_element_type=jnp.float32)
    hidden = jax.nn.silu(pre_stem).astype(jnp.bfloat16)
    pre_mix = jnp.dot(hidden, w_mix, preferred_element_type=jnp.float32)
    mixed = jax.nn.silu(pre_mix).astype(jnp.bfloat16)
    summed = hidden.astype(jnp.float32) + jnp.dot(mixed, w_out, preferred_element_type=jnp.float32)
    pooled = lax.optimization_barrier(jnp.mean(summed.reshape(number, per_cutout, -1), axis=1)).astype(jnp.bfloat16)
    raw_embed = jnp.dot(pooled, w_proj, preferred_element_type=jnp.float32)
    inv_norm = lax.rsqrt(lax.optimization_barrier(jnp.sum(raw_embed * raw_embed, axis=1, keepdims=True)) + norm_eps)
    unit_embed = raw_embed * inv_norm
    return (unit_embed, (patches, pre_stem, hidden, pre_mix, mixed, pooled, unit_embed, inv_norm))

def backward(feature_vector_derivative, saved, w_mix, w_out, w_proj):
    patches, pre_stem, hidden, pre_mix, mixed, pooled, unit_embed, inv_norm = saved
    number = pooled.shape[0]
    per_cutout = patches.shape[0] // number
    channels = hidden.shape[1]
    radial = lax.optimization_barrier(jnp.sum(unit_embed * feature_vector_derivative, axis=1, keepdims=True))
    grad_raw = (inv_norm * (feature_vector_derivative - unit_embed * radial)).astype(jnp.bfloat16)
    grad_proj = first_dot(pooled, grad_raw)
    grad_pool = (concluding_matrix_multiply(grad_raw, w_proj) / per_cutout).astype(jnp.bfloat16)
    mixed_sum = lax.optimization_barrier(jnp.sum(mixed.reshape(number, per_cutout, channels), axis=1, dtype=jnp.float32))
    grad_out = lax.dot_general(mixed_sum, grad_pool.astype(jnp.float32), (((0,), (0,)), ((), ())), precision=lax.Precision.HIGHEST, preferred_element_type=jnp.float32)
    grad_mixed = concluding_matrix_multiply(grad_pool, w_out)
    mix_slope = silu_slope(pre_mix).reshape(number, per_cutout, channels)
    grad_pre_mix = (grad_mixed[:, None, :] * mix_slope).reshape(-1, channels).astype(jnp.bfloat16)
    grad_mix = first_dot(hidden, grad_pre_mix)
    spread_pool = jnp.broadcast_to(grad_pool.astype(jnp.float32)[:, None, :], (number, per_cutout, channels)).reshape(-1, channels)
    grad_hidden = spread_pool + concluding_matrix_multiply(grad_pre_mix, w_mix)
    grad_pre_stem = (grad_hidden * silu_slope(pre_stem)).astype(jnp.bfloat16)
    grad_stem = first_dot(patches, grad_pre_stem)
    return (grad_stem, grad_mix, grad_out, grad_proj)

def contrast(anchor_feature_matrix, whole_feature_matrix, self_pos, pair_pos):
    cosine_affinity_matrix = concluding_matrix_multiply(anchor_feature_matrix, whole_feature_matrix) / logit_divisor_factor
    columns = lax.broadcasted_iota(jnp.int32, cosine_affinity_matrix.shape, 1)
    exp_scores = jnp.where(columns == self_pos[:, None], 0.0, jnp.exp(cosine_affinity_matrix))
    log_total = jnp.log(lax.optimization_barrier(jnp.sum(exp_scores, axis=1)))
    companion_feature_vector = jnp.take(whole_feature_matrix, pair_pos, axis=0).astype(jnp.float32)
    positive_couple_affinity = lax.optimization_barrier(jnp.sum(anchor_feature_matrix.astype(jnp.float32) * companion_feature_vector, axis=1)) / logit_divisor_factor
    return (exp_scores, log_total, companion_feature_vector, log_total - positive_couple_affinity)

def reference(cutouts, counts, partner, w_stem, w_mix, w_out, w_proj):
    node_rank = jnp.arange(NODE_DEV, dtype=jnp.int32)
    block_index = jnp.arange(N_VOL, dtype=jnp.int32)
    node_global = (node_rank[None, :] * N_VOL + block_index[:, None]).astype(jnp.int32)
    self_pos = (block_index[:, None] * NODE_DEV + node_rank[None, :]).astype(jnp.int32)
    grad_sums = (jnp.zeros(w_stem.shape, jnp.float32), jnp.zeros(w_mix.shape, jnp.float32), jnp.zeros(w_out.shape, jnp.float32), jnp.zeros(w_proj.shape, jnp.float32))
    losses = []
    for group in range(N_REP):
        group_counts = counts[group].astype(jnp.int32)
        inclusive = jnp.cumsum(group_counts).astype(jnp.int32)
        offsets = (inclusive - group_counts).astype(jnp.int32)
        owner = lax.optimization_barrier(jnp.sum((inclusive[None, None, :] <= node_global[:, :, None]).astype(jnp.int32), axis=2)).astype(jnp.int32)
        source = (owner * MAXN + node_global - jnp.take(offsets, owner)).astype(jnp.int32)
        group_cutouts = cutouts[group]

        def forward_block(carry, rows):
            unit_embed, saved = encode(jnp.take(group_cutouts, rows, axis=0), w_stem, w_mix, w_out, w_proj)
            return (carry, unit_embed.astype(jnp.bfloat16))
        _, blocks = lax.scan(forward_block, jnp.zeros((), jnp.float32), source)
        whole_feature_matrix = blocks.reshape(NODES, -1)
        pair_global = jnp.take(partner[group].astype(jnp.int32), node_global)
        pair_pos = (pair_global % N_VOL * NODE_DEV + pair_global // N_VOL).astype(jnp.int32)

        def total_block(carry, inputs):
            anchor_feature_matrix, self_rows, pair_rows = inputs
            _, log_total, _, row_loss = contrast(anchor_feature_matrix, whole_feature_matrix, self_rows, pair_rows)
            return (carry, (log_total, row_loss))
        _, (log_totals, group_loss) = lax.scan(total_block, jnp.zeros((), jnp.float32), (blocks, self_pos, pair_pos))
        all_totals = log_totals.reshape(NODES)

        def grad_block(carry, inputs):
            anchor_feature_matrix, self_rows, pair_rows, rows = inputs
            exp_scores, log_total, companion_feature_vector, _ = contrast(anchor_feature_matrix, whole_feature_matrix, self_rows, pair_rows)
            row_weight = (exp_scores * jnp.exp(-log_total)[:, None]).astype(jnp.bfloat16)
            column_weight = (exp_scores * jnp.exp(-all_totals)[None, :]).astype(jnp.bfloat16)
            horizontal_objective_term = jnp.dot(row_weight, whole_feature_matrix, preferred_element_type=jnp.float32)
            vertical_objective_term = jnp.dot(column_weight, whole_feature_matrix, preferred_element_type=jnp.float32)
            feature_vector_derivative = (horizontal_objective_term + vertical_objective_term - 2.0 * companion_feature_vector) / logit_divisor_factor
            _, saved = encode(jnp.take(group_cutouts, rows, axis=0), w_stem, w_mix, w_out, w_proj)
            grads = backward(feature_vector_derivative, saved, w_mix, w_out, w_proj)
            return (jax.tree.map(jnp.add, carry, grads), None)
        grad_sums, _ = lax.scan(grad_block, grad_sums, (blocks, self_pos, pair_pos, source))
        losses.append(group_loss)
    updates = [summed_grad * lax.rsqrt(jnp.mean(summed_grad * summed_grad) + rms_eps) for summed_grad in grad_sums]
    return (updates[0], updates[1], updates[2], updates[3], jnp.stack(losses))
```

```python
import functools

import jax
import jax.numpy as jnp
from jax import lax
from jax.experimental import pallas as pl
from jax.experimental.pallas import tpu as pltpu
from jax.sharding import PartitionSpec as P

MESH = pl.DeviceIdType.MESH
F32 = jnp.float32
BF16 = jnp.bfloat16
HIGHEST = lax.Precision.HIGHEST

NZ, NP, NY = 16, 8, 4
NV = NZ * NP
NQ = NP * NY
C, E, VOX, PATCHES = 128, 64, 64, 64
SLOTS, HALF = 32, 16
NODES = 2048
DEAD = NV * SLOTS - NODES
NEAR = 4
PAIRS = PATCHES // 2
ROWS = PAIRS * SLOTS
CHUNK = 256
LINE = NZ * HALF
TEMPERATURE = 0.2
LOG2E = 1.4426950408889634
SCALE = LOG2E / TEMPERATURE
EPS = 1e-6


def iota(shape, dim):
    return lax.broadcasted_iota(jnp.int32, shape, dim)


def dot(a, b, precision=None):
    return lax.dot_general(a, b, (((1,), (0,)), ((), ())), precision=precision, preferred_element_type=F32)


def dot_nt(a, b):
    return lax.dot_general(a, b, (((1,), (1,)), ((), ())), preferred_element_type=F32)


def dot_tn(a, b, precision=None):
    return lax.dot_general(a, b, (((0,), (0,)), ((), ())), precision=precision, preferred_element_type=F32)


def sigmoid(v):
    return 1.0 / (1.0 + jnp.exp(-v))


def twice(v):
    return jnp.concatenate([v, v], axis=1)


def fold(v):
    half = v.shape[1] // 2
    return v[:, :half] + v[:, half:]


def block_diagonal(w):
    zero = jnp.zeros_like(w)
    return jnp.concatenate(
        [jnp.concatenate([w, zero], axis=1), jnp.concatenate([zero, w], axis=1)], axis=0
    )


def kernel(
    cut_ref, count_ref, partner_ref, stem_ref, mix_ref, out_ref, proj_ref,
    up_stem_ref, up_mix_ref, up_out_ref, up_proj_ref, loss_ref,
    x_s, hid_s, slope1_s, slope2_s, xt_s, ht_s,
    emb_s, cnt_s, tot_s, part_s, gath_s, zed_s, fin_s,
    send_sem, recv_sem,
):
    vol = lax.axis_index("vol")
    rep = lax.axis_index("rep")
    z = vol // NP
    p = lax.rem(vol, NP)
    q = rep * NP + p

    def z_peer(step):
        return (lax.rem(z + step + NZ, NZ) * NP + p, rep)

    def p_peer(step):
        return (z * NP + lax.rem(p + step, NP), rep)

    def q_peer(other):
        return (z * NP + lax.rem(other, NP), other // NP)

    def send(src, dst, kind, device):
        pltpu.make_async_remote_copy(
            src_ref=src, dst_ref=dst, send_sem=send_sem.at[kind], recv_sem=recv_sem.at[kind],
            device_id=device, device_id_type=MESH,
        ).start()

    def arrived(ref, kind):
        pltpu.make_async_copy(ref, ref, recv_sem.at[kind]).wait()

    def sent(ref, kind):
        pltpu.make_async_copy(ref, ref, send_sem.at[kind]).wait()

    barrier = pltpu.get_barrier_semaphore()
    greeted = 0
    for step in range(NEAR, 0, -1):
        for sign in (1, -1):
            pl.semaphore_signal(barrier, inc=1, device_id=z_peer(sign * step), device_id_type=MESH)
            greeted += 1
    for step in range(1, NY):
        pl.semaphore_signal(
            barrier, inc=1, device_id=(vol, lax.rem(rep + step, NY)), device_id_type=MESH
        )
        greeted += 1
    for step in range(1, NP):
        pl.semaphore_signal(barrier, inc=1, device_id=p_peer(step), device_id_type=MESH)
        greeted += 1

    count = count_ref[0, 0]
    cnt_s[p, NEAR] = jnp.full((1, 128), count, jnp.int32).astype(F32)
    w_stem2 = block_diagonal(stem_ref[...])
    w_mix2 = block_diagonal(mix_ref[...])
    for pair in range(PAIRS):
        x_s[pair * SLOTS:(pair + 1) * SLOTS, :] = cut_ref[:, pair * 128:(pair + 1) * 128]

    def forward(step, sums):
        hid_sum, mix_sum = sums
        rows = pl.ds(pl.multiple_of(step * CHUNK, CHUNK), CHUNK)
        pre1 = dot(x_s[rows, :], w_stem2)
        sig1 = sigmoid(pre1)
        hidden = (pre1 * sig1).astype(BF16)
        slope1_s[rows, :] = sig1 * (1.0 + pre1 * (1.0 - sig1))
        hid_s[rows, :] = hidden
        pre2 = dot(hidden, w_mix2)
        sig2 = sigmoid(pre2)
        mixed = (pre2 * sig2).astype(BF16)
        slope2_s[rows, :] = sig2 * (1.0 + pre2 * (1.0 - sig2))
        hid_sum = hid_sum + jnp.sum(hidden.astype(F32).reshape(CHUNK // SLOTS, SLOTS, 2 * C), axis=0)
        mix_sum = mix_sum + jnp.sum(mixed.astype(F32).reshape(CHUNK // SLOTS, SLOTS, 2 * C), axis=0)
        return hid_sum, mix_sum

    start = jnp.zeros((SLOTS, 2 * C), F32)
    hid_sum, mix_sum = lax.fori_loop(0, ROWS // CHUNK, forward, (start, start))
    hid_sum, mix_sum = fold(hid_sum), fold(mix_sum)
    w_out = out_ref[...]
    pooled = ((hid_sum + dot(mix_sum, w_out.astype(F32), HIGHEST)) * (1.0 / PATCHES)).astype(BF16)
    raw = dot(pooled, proj_ref[...])
    inv_norm = lax.rsqrt(jnp.sum(raw * raw, axis=1, keepdims=True) + EPS)
    unit = raw * inv_norm
    live = iota((SLOTS, E), 0) < count
    embed = jnp.where(live, unit, 0.0).astype(BF16)
    emb_s[p, NEAR] = jnp.concatenate([embed[:HALF], embed[HALF:]], axis=1)

    pl.semaphore_wait(barrier, greeted)

    own = emb_s.at[p, NEAR]
    own_count = cnt_s.at[p, NEAR]
    for step in range(NEAR, 0, -1):
        for sign in (1, -1):
            send(own, emb_s.at[p, NEAR - sign * step], 0, z_peer(sign * step))
    for step in range(NEAR, 0, -1):
        for sign in (1, -1):
            send(own_count, cnt_s.at[p, NEAR - sign * step], 1, z_peer(sign * step))

    xt_s[...] = x_s[...].T
    ht_s[...] = hid_s[...].T
    lane = iota((HALF, 128), 1)
    zero_half = jnp.zeros((HALF, E), BF16)
    zero_slots = jnp.zeros((SLOTS, E), BF16)
    anchors = jnp.concatenate(
        [jnp.concatenate([embed, zero_slots], axis=1), jnp.concatenate([zero_slots, embed], axis=1)], axis=0
    )

    arrived(emb_s.at[0, 0:2 * NEAR], 0)
    far = NZ - 2 * NEAR - 1
    send(emb_s.at[p, NEAR + 1:2 * NEAR + 1], emb_s.at[p, 2 * NEAR + 1:3 * NEAR + 1], 2, z_peer(-NEAR))
    send(emb_s.at[p, 1:NEAR], emb_s.at[p, 3 * NEAR + 1:4 * NEAR], 2, z_peer(NEAR))
    arrived(cnt_s.at[0, 0:2 * NEAR], 1)
    send(cnt_s.at[p, NEAR + 1:2 * NEAR + 1], cnt_s.at[p, 2 * NEAR + 1:3 * NEAR + 1], 3, z_peer(-NEAR))
    send(cnt_s.at[p, 1:NEAR], cnt_s.at[p, 3 * NEAR + 1:4 * NEAR], 3, z_peer(NEAR))
    near_block = emb_s.at[p, 0:2 * NEAR + 1]
    for step in range(1, NP):
        send(near_block, near_block, 4, p_peer(step))
    arrived(emb_s.at[0, 0:far], 2)
    far_block = emb_s.at[p, 2 * NEAR + 1:NZ]
    for step in range(1, NP):
        send(far_block, far_block, 5, p_peer(step))
    arrived(cnt_s.at[0, 0:far], 3)
    count_block = cnt_s.at[p]
    for step in range(1, NP):
        send(count_block, count_block, 6, p_peer(step))

    line = emb_s[p].reshape(LINE, 128)
    low = iota((LINE, 128), 1) < E
    turned = jnp.concatenate([line[:, E:], line[:, :E]], axis=1)
    none = jnp.zeros_like(line)
    columns = jnp.concatenate(
        [
            jnp.where(low, line, none), jnp.where(low, turned, none),
            jnp.where(low, none, turned), jnp.where(low, none, line),
        ],
        axis=0,
    )

    def scores(part):
        block = emb_s[part].reshape(LINE, 128)
        return jnp.exp2(dot_nt(block, columns) * SCALE)

    def add_rows(e):
        return jnp.sum(e.reshape(LINE // 8, 8, 4 * LINE), axis=0)

    col = iota((LINE, 4 * LINE), 1)
    row = iota((LINE, 4 * LINE), 0)
    self_score = (col == row) | (col == row + 3 * LINE)
    total = add_rows(jnp.where(self_score, 0.0, scores(p)))
    arrived(emb_s.at[0:NP - 1, 0:2 * NEAR + 1], 4)
    arrived(emb_s.at[0:NP - 1, 0:far], 5)

    def other(step, total):
        return total + add_rows(scores(lax.rem(p + step, NP)))

    total = lax.fori_loop(1, NP, other, total)
    line_sum = fold(jnp.sum(total, axis=0, keepdims=True)) - float(DEAD)
    tot_s[p] = jnp.concatenate([line_sum[:, :LINE], line_sum[:, LINE:]], axis=0)
    own_total = tot_s.at[p]
    for step in range(1, NP):
        send(own_total, own_total, 7, p_peer(step))

    every = emb_s[...].reshape(NP * LINE, 128)
    wide = NP * LINE
    exps = jnp.exp2(dot_nt(anchors, every) * SCALE)
    row = iota((2 * SLOTS, wide), 0)
    col = iota((2 * SLOTS, wide), 1)
    slot = lax.rem(row, SLOTS)
    self_score = (row // SLOTS == slot // HALF) & (col == p * LINE + NEAR * HALF + lax.rem(slot, HALF))
    exps = jnp.where(self_score, 0.0, exps)
    row_sum = jnp.sum(exps, axis=1, keepdims=True)
    own_sum = row_sum[:SLOTS] + row_sum[SLOTS:] - float(DEAD)
    own_inv = 1.0 / own_sum
    row_weight = (exps * jnp.concatenate([own_inv, own_inv], axis=0)).astype(BF16)

    arrived(cnt_s.at[0:NP - 1], 6)
    counts = cnt_s[...]
    by_plane = jnp.sum(counts, axis=0)

    def place(relative):
        return lax.rem(z + relative + NZ - NEAR, NZ)

    plane_row = place(iota((NZ, 1, 128), 0))
    numbers = [[], []]
    own_offset = jnp.sum(jnp.where(plane_row < z, by_plane, 0.0), axis=0)
    before = [own_offset]
    for group in range(2):
        relative = iota((NZ, 1, 128), 2) // HALF + group * (NZ // 2)
        offset = jnp.sum(jnp.where(plane_row < place(relative), by_plane, 0.0), axis=0)
        inside = lax.rem(iota((1, 128), 1), HALF).astype(F32)
        for part in range(NP):
            amount = jnp.sum(jnp.where(iota((NZ, 1, 128), 0) == relative, counts[part], 0.0), axis=0)
            for half in range(2):
                position = inside + float(half * HALF)
                numbers[half].append((part, group, jnp.where(position < amount, offset + position, -1.0)))
            offset = offset + amount
    for part in range(NP):
        own_offset = own_offset + jnp.where(part < p, counts[part, NEAR], 0.0)
    number = []
    for half in range(2):
        ordered = sorted(numbers[half], key=lambda item: item[:2])
        number.append(jnp.concatenate([value for _, _, value in ordered], axis=1))

    table = partner_ref[...].astype(F32)
    node = iota((1, NODES), 1).astype(F32)
    own_number = own_offset[:, :1] + iota((SLOTS, 1), 0).astype(F32)
    out_number = (iota((HALF, 1), 0) * NV + vol).astype(F32)
    wanted = jnp.concatenate([own_number, out_number], axis=0)
    mates = jnp.sum(jnp.where(node == wanted, table, 0.0), axis=1, keepdims=True)
    pick = jnp.concatenate([mates, out_number], axis=0)
    picked = [(number[half] == pick) for half in range(2)]
    ones = [jnp.where(match, 1.0, 0.0).astype(BF16) for match in picked]
    first = dot(jnp.concatenate([row_weight] + ones, axis=0), every)
    rows_term = first[:SLOTS, :E] + first[SLOTS:2 * SLOTS, E:]
    n_pick = SLOTS + 2 * HALF
    chosen = first[2 * SLOTS:2 * SLOTS + n_pick, :E] + first[2 * SLOTS + n_pick:, E:]
    companion = chosen[:SLOTS]

    arrived(tot_s.at[0:NP - 1], 7)
    sums = [
        jnp.concatenate([tot_s[part, half:half + 1, :] for part in range(NP)], axis=1) for half in range(2)
    ]
    col_weight = jnp.concatenate(
        [exps[half * SLOTS:(half + 1) * SLOTS] * (1.0 / sums[half]) for half in range(2)], axis=0
    ).astype(BF16)
    second = dot(col_weight, every)
    cols_term = second[:SLOTS, :E] + second[SLOTS:, E:]

    d_embed = (rows_term + cols_term - 2.0 * companion) * (1.0 / TEMPERATURE)
    radial = jnp.sum(unit * d_embed, axis=1, keepdims=True)
    d_raw = jnp.where(live, inv_norm * (d_embed - unit * radial), 0.0).astype(BF16)
    g_proj = dot_tn(d_raw, pooled)
    d_sum = (dot_nt(d_raw, proj_ref[...]) * (1.0 / PATCHES)).astype(BF16)
    d_sum32 = d_sum.astype(F32)
    g_out = dot_tn(mix_sum, d_sum32, HIGHEST)
    d_mixed = twice(dot_nt(d_sum, w_out))
    d_spread = twice(d_sum32)

    for tile in range(NP * 2):
        part_s[16 + tile, 0:8, :] = g_out[tile * 8:(tile + 1) * 8]
        part_s[16 + tile, 8:12, :] = g_proj[tile * 4:(tile + 1) * 4]

    g_mix = jnp.zeros((2 * C, 2 * C), F32)
    g_stem = jnp.zeros((2 * VOX, 2 * C), F32)
    for step in range(ROWS // CHUNK):
        rows = slice(step * CHUNK, (step + 1) * CHUNK)
        shape = (CHUNK // SLOTS, SLOTS, 2 * C)
        d_pre2 = (slope2_s[rows, :].reshape(shape) * d_mixed[None]).reshape(CHUNK, 2 * C).astype(BF16)
        g_mix = g_mix + dot(ht_s[:, rows], d_pre2)
        d_hid = (dot_nt(d_pre2, w_mix2).reshape(shape) + d_spread[None]).reshape(CHUNK, 2 * C)
        d_pre1 = (d_hid * slope1_s[rows, :]).astype(BF16)
        g_stem = g_stem + dot(xt_s[:, rows], d_pre1)
    g_mix = g_mix[:C, :C] + g_mix[C:, C:]
    g_stem = g_stem[:VOX, :C] + g_stem[VOX:, C:]
    for tile in range(NP * 2):
        part_s[tile, 0:8, :] = g_mix[tile * 8:(tile + 1) * 8]
        part_s[tile, 8:12, :] = g_stem[tile * 4:(tile + 1) * 4]

    def scatter(step, carry):
        to = lax.rem(q + step, NQ)
        send(part_s.at[to], gath_s.at[q], 8, q_peer(to))
        return carry

    lax.fori_loop(1, NQ, scatter, 0)
    gath_s[q] = part_s[q]

    out_sum = jnp.zeros((HALF, 1), F32)
    for half in range(2):
        hit = picked[half][SLOTS + HALF:]
        out_sum = out_sum + jnp.sum(jnp.where(hit, sums[half], 0.0), axis=1, keepdims=True)
    affinity = jnp.sum(chosen[SLOTS:SLOTS + HALF] * chosen[SLOTS + HALF:], axis=1, keepdims=True)
    loss = jnp.log(out_sum) - affinity * (1.0 / TEMPERATURE)
    square = iota((HALF, HALF), 0) == iota((HALF, HALF), 1)
    loss_ref[...] = jnp.sum(jnp.where(square, loss, 0.0), axis=0, keepdims=True)

    arrived(gath_s.at[0:NQ - 1], 8)
    zed_s[z] = jnp.sum(gath_s[...], axis=0)
    for step in range(NZ // 2, 0, -1):
        for sign in (1, -1):
            if step < NZ // 2 or sign == 1:
                send(zed_s.at[z], zed_s.at[z], 9, z_peer(sign * step))
    arrived(zed_s.at[0:NZ - 1], 9)
    fin_s[q] = jnp.sum(zed_s[...], axis=0)

    def spread(step, carry):
        send(fin_s.at[q], fin_s.at[q], 10, q_peer(lax.rem(q + step, NQ)))
        return carry

    lax.fori_loop(1, NQ, spread, 0)
    arrived(fin_s.at[0:NQ - 1], 10)

    def normal(g):
        return g * lax.rsqrt(jnp.mean(g * g) + EPS)

    up_mix_ref[...] = normal(fin_s[0:16, 0:8, :].reshape(C, C))
    up_out_ref[...] = normal(fin_s[16:32, 0:8, :].reshape(C, C))
    up_stem_ref[...] = normal(jnp.concatenate([fin_s[tile, 8:12, :] for tile in range(16)], axis=0))
    up_proj_ref[...] = normal(jnp.concatenate([fin_s[16 + tile, 8:12, :] for tile in range(16)], axis=0)).T

    sent(emb_s.at[0, 0:2 * NEAR], 0)
    sent(cnt_s.at[0, 0:2 * NEAR], 1)
    sent(emb_s.at[0, 0:far], 2)
    sent(cnt_s.at[0, 0:far], 3)
    sent(emb_s.at[0:NP - 1, 0:2 * NEAR + 1], 4)
    sent(emb_s.at[0:NP - 1, 0:far], 5)
    sent(cnt_s.at[0:NP - 1], 6)
    sent(tot_s.at[0:NP - 1], 7)
    sent(gath_s.at[0:NQ - 1], 8)
    sent(zed_s.at[0:NZ - 1], 9)
    sent(fin_s.at[0:NQ - 1], 10)


def on_device(cutouts, counts, partner, w_stem, w_mix, w_out, w_proj):
    vmem = pl.BlockSpec(memory_space=pltpu.VMEM)
    outs = pl.pallas_call(
        kernel,
        out_shape=(
            jax.ShapeDtypeStruct((VOX, C), F32),
            jax.ShapeDtypeStruct((C, C), F32),
            jax.ShapeDtypeStruct((C, C), F32),
            jax.ShapeDtypeStruct((C, E), F32),
            jax.ShapeDtypeStruct((1, HALF), F32),
        ),
        in_specs=[vmem, pl.BlockSpec(memory_space=pltpu.SMEM)] + [vmem] * 5,
        out_specs=(vmem,) * 5,
        scratch_shapes=[
            pltpu.VMEM((ROWS, 128), BF16),
            pltpu.VMEM((ROWS, 2 * C), BF16),
            pltpu.VMEM((ROWS, 2 * C), F32),
            pltpu.VMEM((ROWS, 2 * C), F32),
            pltpu.VMEM((128, ROWS), BF16),
            pltpu.VMEM((2 * C, ROWS), BF16),
            pltpu.VMEM((NP, NZ, HALF, 128), BF16),
            pltpu.VMEM((NP, NZ, 1, 128), F32),
            pltpu.VMEM((NP, 2, LINE), F32),
            pltpu.VMEM((NQ, 12, 128), F32),
            pltpu.VMEM((NQ, 12, 128), F32),
            pltpu.VMEM((NZ, 12, 128), F32),
            pltpu.VMEM((NQ, 12, 128), F32),
            pltpu.SemaphoreType.DMA((11,)),
            pltpu.SemaphoreType.DMA((11,)),
        ],
        compiler_params=pltpu.CompilerParams(
            collective_id=0, has_side_effects=True, vmem_limit_bytes=40 * 1024 * 1024
        ),
    )(cutouts[0], counts, partner, w_stem, w_mix, w_out, w_proj)
    return outs[:4] + (outs[4][None],)


def solution(mesh):
    in_specs = (P("rep", "vol", None), P("rep", "vol"), P("rep", None), P(), P(), P(), P())
    out_specs = (P(), P(), P(), P(), P("rep", "vol", None))
    return jax.shard_map(
        on_device, mesh=mesh, in_specs=in_specs, out_specs=out_specs, check_vma=False
    )
```

```python
import functools

import jax
import jax.numpy as jnp
from jax import lax
from jax.experimental import pallas as pl
from jax.experimental.pallas import tpu as pltpu
from jax.sharding import PartitionSpec as P

MESH = pl.DeviceIdType.MESH
F32 = jnp.float32
BF16 = jnp.bfloat16
HIGHEST = lax.Precision.HIGHEST

NZ, NP, NY = 16, 8, 4
NV = NZ * NP
NQ = NP * NY
C, E, VOX, PATCHES = 128, 64, 64, 64
SLOTS, HALF = 32, 16
NODES = 2048
DEAD = NV * SLOTS - NODES
NEAR = 4
PAIRS = PATCHES // 2
ROWS = PAIRS * SLOTS
CHUNK = 256
LINE = NZ * HALF
TEMPERATURE = 0.2
LOG2E = 1.4426950408889634
SCALE = LOG2E / TEMPERATURE
EPS = 1e-6


def iota(shape, dim):
    return lax.broadcasted_iota(jnp.int32, shape, dim)


def dot(a, b, precision=None):
    return lax.dot_general(a, b, (((1,), (0,)), ((), ())), precision=precision, preferred_element_type=F32)


def dot_nt(a, b):
    return lax.dot_general(a, b, (((1,), (1,)), ((), ())), preferred_element_type=F32)


def dot_tn(a, b, precision=None):
    return lax.dot_general(a, b, (((0,), (0,)), ((), ())), precision=precision, preferred_element_type=F32)


def sigmoid(v):
    return 1.0 / (1.0 + jnp.exp(-v))


def twice(v):
    return jnp.concatenate([v, v], axis=1)


def fold(v):
    half = v.shape[1] // 2
    return v[:, :half] + v[:, half:]


def block_diagonal(w):
    zero = jnp.zeros_like(w)
    return jnp.concatenate(
        [jnp.concatenate([w, zero], axis=1), jnp.concatenate([zero, w], axis=1)], axis=0
    )


def kernel(
    cut_hbm, count_hbm, partner_hbm, stem_hbm, mix_hbm, out_hbm, proj_hbm,
    up_ref, loss_ref,
    cut_ref, count_ref, partner_ref, stem_ref, mix_ref, out_ref, proj_ref, load_sem,
    x_s, hid_s, slope1_s, slope2_s, xt_s, ht_s,
    emb_s, cnt_s, tot_s, part_s, gath_s, zed_s, fin_s,
    send_sem, recv_sem,
):
    vol = lax.axis_index("vol")
    rep = lax.axis_index("rep")
    z = vol // NP
    p = lax.rem(vol, NP)
    q = rep * NP + p

    def z_peer(step):
        return (lax.rem(z + step + NZ, NZ) * NP + p, rep)

    def p_peer(step):
        return (z * NP + lax.rem(p + step, NP), rep)

    def q_peer(other):
        return (z * NP + lax.rem(other, NP), other // NP)

    def send(src, dst, kind, device):
        pltpu.make_async_remote_copy(
            src_ref=src, dst_ref=dst, send_sem=send_sem.at[kind], recv_sem=recv_sem.at[kind],
            device_id=device, device_id_type=MESH,
        ).start()

    def arrived(ref, kind):
        pltpu.make_async_copy(ref, ref, recv_sem.at[kind]).wait()

    def sent(ref, kind):
        pltpu.make_async_copy(ref, ref, send_sem.at[kind]).wait()

    loads = [
        pltpu.make_async_copy(source, target, load_sem.at[number])
        for number, (source, target) in enumerate([
            (cut_hbm, cut_ref), (stem_hbm, stem_ref), (mix_hbm, mix_ref), (count_hbm, count_ref),
            (out_hbm, out_ref), (proj_hbm, proj_ref), (partner_hbm, partner_ref),
        ])
    ]
    for load in loads:
        load.start()

    barrier = pltpu.get_barrier_semaphore()
    greeted = 0
    for step in range(NEAR, 0, -1):
        for sign in (1, -1):
            pl.semaphore_signal(barrier, inc=1, device_id=z_peer(sign * step), device_id_type=MESH)
            greeted += 1
    for step in range(1, NY):
        pl.semaphore_signal(
            barrier, inc=1, device_id=(vol, lax.rem(rep + step, NY)), device_id_type=MESH
        )
        greeted += 1
    for step in range(1, NP):
        pl.semaphore_signal(barrier, inc=1, device_id=p_peer(step), device_id_type=MESH)
        greeted += 1

    for load in loads:
        load.wait()
    count = count_ref[...]
    cnt_s[p, NEAR] = jnp.broadcast_to(count, (1, 128)).astype(F32)
    w_stem2 = block_diagonal(stem_ref[...])
    w_mix2 = block_diagonal(mix_ref[...])
    for pair in range(PAIRS):
        x_s[pair * SLOTS:(pair + 1) * SLOTS, :] = cut_ref[:, pair * 128:(pair + 1) * 128]

    def forward(step, sums):
        hid_sum, mix_sum = sums
        rows = pl.ds(pl.multiple_of(step * CHUNK, CHUNK), CHUNK)
        pre1 = dot(x_s[rows, :], w_stem2)
        sig1 = sigmoid(pre1)
        hidden = (pre1 * sig1).astype(BF16)
        slope1_s[rows, :] = sig1 * (1.0 + pre1 * (1.0 - sig1))
        hid_s[rows, :] = hidden
        pre2 = dot(hidden, w_mix2)
        sig2 = sigmoid(pre2)
        mixed = (pre2 * sig2).astype(BF16)
        slope2_s[rows, :] = sig2 * (1.0 + pre2 * (1.0 - sig2))
        hid_sum = hid_sum + jnp.sum(hidden.astype(F32).reshape(CHUNK // SLOTS, SLOTS, 2 * C), axis=0)
        mix_sum = mix_sum + jnp.sum(mixed.astype(F32).reshape(CHUNK // SLOTS, SLOTS, 2 * C), axis=0)
        return hid_sum, mix_sum

    start = jnp.zeros((SLOTS, 2 * C), F32)
    hid_sum, mix_sum = lax.fori_loop(0, ROWS // CHUNK, forward, (start, start))
    hid_sum, mix_sum = fold(hid_sum), fold(mix_sum)
    w_out = out_ref[...]
    pooled = ((hid_sum + dot(mix_sum, w_out.astype(F32), HIGHEST)) * (1.0 / PATCHES)).astype(BF16)
    raw = dot_nt(pooled, proj_ref[...])
    inv_norm = lax.rsqrt(jnp.sum(raw * raw, axis=1, keepdims=True) + EPS)
    unit = raw * inv_norm
    live = iota((SLOTS, E), 0) < count
    embed = jnp.where(live, unit, 0.0).astype(BF16)
    emb_s[p, NEAR] = jnp.concatenate([embed[:HALF], embed[HALF:]], axis=1)

    pl.semaphore_wait(barrier, greeted)

    own = emb_s.at[p, NEAR]
    own_count = cnt_s.at[p, NEAR]
    for step in range(NEAR, 0, -1):
        for sign in (1, -1):
            send(own, emb_s.at[p, NEAR - sign * step], 0, z_peer(sign * step))
    for step in range(NEAR, 0, -1):
        for sign in (1, -1):
            send(own_count, cnt_s.at[p, NEAR - sign * step], 1, z_peer(sign * step))

    xt_s[...] = x_s[...].T
    ht_s[...] = hid_s[...].T
    lane = iota((HALF, 128), 1)
    zero_half = jnp.zeros((HALF, E), BF16)
    zero_slots = jnp.zeros((SLOTS, E), BF16)
    anchors = jnp.concatenate(
        [jnp.concatenate([embed, zero_slots], axis=1), jnp.concatenate([zero_slots, embed], axis=1)], axis=0
    )

    arrived(emb_s.at[0, 0:2 * NEAR], 0)
    far = NZ - 2 * NEAR - 1
    send(emb_s.at[p, NEAR + 1:2 * NEAR + 1], emb_s.at[p, 2 * NEAR + 1:3 * NEAR + 1], 2, z_peer(-NEAR))
    send(emb_s.at[p, 1:NEAR], emb_s.at[p, 3 * NEAR + 1:4 * NEAR], 2, z_peer(NEAR))
    arrived(cnt_s.at[0, 0:2 * NEAR], 1)
    send(cnt_s.at[p, NEAR + 1:2 * NEAR + 1], cnt_s.at[p, 2 * NEAR + 1:3 * NEAR + 1], 3, z_peer(-NEAR))
    send(cnt_s.at[p, 1:NEAR], cnt_s.at[p, 3 * NEAR + 1:4 * NEAR], 3, z_peer(NEAR))
    near_block = emb_s.at[p, 0:2 * NEAR + 1]
    for step in range(1, NP):
        send(near_block, near_block, 4, p_peer(step))
    arrived(emb_s.at[0, 0:far], 2)
    far_block = emb_s.at[p, 2 * NEAR + 1:NZ]
    for step in range(1, NP):
        send(far_block, far_block, 5, p_peer(step))
    arrived(cnt_s.at[0, 0:far], 3)
    count_block = cnt_s.at[p]
    for step in range(1, NP):
        send(count_block, count_block, 6, p_peer(step))

    line = emb_s[p].reshape(LINE, 128)
    low = iota((LINE, 128), 1) < E
    turned = jnp.concatenate([line[:, E:], line[:, :E]], axis=1)
    none = jnp.zeros_like(line)
    columns = jnp.concatenate(
        [
            jnp.where(low, line, none), jnp.where(low, turned, none),
            jnp.where(low, none, turned), jnp.where(low, none, line),
        ],
        axis=0,
    )

    def add_rows(e):
        return jnp.sum(e.reshape(e.shape[0] // 8, 8, 4 * LINE), axis=0)

    col = iota((LINE, 4 * LINE), 1)
    row = iota((LINE, 4 * LINE), 0)
    self_score = (col == row) | (col == row + 3 * LINE)
    total = add_rows(jnp.where(self_score, 0.0, jnp.exp2(dot_nt(line, columns) * SCALE)))

    def other(first, last):
        def add(step, total):
            block = emb_s[lax.rem(p + step, NP), first:last].reshape((last - first) * HALF, 128)
            return total + add_rows(jnp.exp2(dot_nt(block, columns) * SCALE))
        return add

    arrived(emb_s.at[0:NP - 1, 0:2 * NEAR + 1], 4)
    total = lax.fori_loop(1, NP, other(0, 2 * NEAR + 1), total)
    arrived(emb_s.at[0:NP - 1, 0:far], 5)
    total = lax.fori_loop(1, NP, other(2 * NEAR + 1, NZ), total)
    line_sum = fold(jnp.sum(total, axis=0, keepdims=True)) - float(DEAD)
    tot_s[p] = jnp.concatenate([line_sum[:, :LINE], line_sum[:, LINE:]], axis=0)
    own_total = tot_s.at[p]
    for step in range(1, NP):
        send(own_total, own_total, 7, p_peer(step))

    every = emb_s[...].reshape(NP * LINE, 128)
    wide = NP * LINE
    exps = jnp.exp2(dot_nt(anchors, every) * SCALE)
    row = iota((2 * SLOTS, wide), 0)
    col = iota((2 * SLOTS, wide), 1)
    slot = lax.rem(row, SLOTS)
    self_score = (row // SLOTS == slot // HALF) & (col == p * LINE + NEAR * HALF + lax.rem(slot, HALF))
    exps = jnp.where(self_score, 0.0, exps)
    row_sum = jnp.sum(exps, axis=1, keepdims=True)
    own_sum = row_sum[:SLOTS] + row_sum[SLOTS:] - float(DEAD)
    own_inv = 1.0 / own_sum
    row_weight = (exps * jnp.concatenate([own_inv, own_inv], axis=0)).astype(BF16)

    arrived(cnt_s.at[0:NP - 1], 6)
    counts = cnt_s[...]
    by_plane = jnp.sum(counts, axis=0)

    def place(relative):
        return lax.rem(z + relative + NZ - NEAR, NZ)

    plane_row = place(iota((NZ, 1, 128), 0))
    numbers = [[], []]
    own_offset = jnp.sum(jnp.where(plane_row < z, by_plane, 0.0), axis=0)
    before = [own_offset]
    for group in range(2):
        relative = iota((NZ, 1, 128), 2) // HALF + group * (NZ // 2)
        offset = jnp.sum(jnp.where(plane_row < place(relative), by_plane, 0.0), axis=0)
        inside = lax.rem(iota((1, 128), 1), HALF).astype(F32)
        for part in range(NP):
            amount = jnp.sum(jnp.where(iota((NZ, 1, 128), 0) == relative, counts[part], 0.0), axis=0)
            for half in range(2):
                position = inside + float(half * HALF)
                numbers[half].append((part, group, jnp.where(position < amount, offset + position, -1.0)))
            offset = offset + amount
    for part in range(NP):
        own_offset = own_offset + jnp.where(part < p, counts[part, NEAR], 0.0)
    number = []
    for half in range(2):
        ordered = sorted(numbers[half], key=lambda item: item[:2])
        number.append(jnp.concatenate([value for _, _, value in ordered], axis=1))

    table = partner_ref[...].astype(F32)
    node = iota((1, NODES), 1).astype(F32)
    own_number = own_offset[:, :1] + iota((SLOTS, 1), 0).astype(F32)
    out_number = (iota((HALF, 1), 0) * NV + vol).astype(F32)
    wanted = jnp.concatenate([own_number, out_number], axis=0)
    mates = jnp.sum(jnp.where(node == wanted, table, 0.0), axis=1, keepdims=True)
    pick = jnp.concatenate([mates, out_number], axis=0)
    picked = [(number[half] == pick) for half in range(2)]
    ones = [jnp.where(match, 1.0, 0.0).astype(BF16) for match in picked]
    first = dot(jnp.concatenate([row_weight] + ones, axis=0), every)
    rows_term = first[:SLOTS, :E] + first[SLOTS:2 * SLOTS, E:]
    n_pick = SLOTS + 2 * HALF
    chosen = first[2 * SLOTS:2 * SLOTS + n_pick, :E] + first[2 * SLOTS + n_pick:, E:]
    companion = chosen[:SLOTS]

    arrived(tot_s.at[0:NP - 1], 7)
    sums = [
        jnp.concatenate([tot_s[part, half:half + 1, :] for part in range(NP)], axis=1) for half in range(2)
    ]
    col_weight = jnp.concatenate(
        [exps[half * SLOTS:(half + 1) * SLOTS] * (1.0 / sums[half]) for half in range(2)], axis=0
    ).astype(BF16)
    second = dot(col_weight, every)
    cols_term = second[:SLOTS, :E] + second[SLOTS:, E:]

    d_embed = (rows_term + cols_term - 2.0 * companion) * (1.0 / TEMPERATURE)
    radial = jnp.sum(unit * d_embed, axis=1, keepdims=True)
    d_raw = jnp.where(live, inv_norm * (d_embed - unit * radial), 0.0).astype(BF16)
    g_proj = dot_tn(d_raw, pooled)
    d_sum = (dot(d_raw, proj_ref[...]) * (1.0 / PATCHES)).astype(BF16)
    d_sum32 = d_sum.astype(F32)
    g_out = dot_tn(mix_sum, d_sum32, HIGHEST)
    d_mixed = twice(dot_nt(d_sum, w_out))
    d_spread = twice(d_sum32)

    def scatter(first):
        def one(step, carry):
            to = first + lax.rem(q + step, NQ // 2)
            send(part_s.at[to], gath_s.at[q], 8, q_peer(to))
            return carry

        inside = (q // (NQ // 2) == first // (NQ // 2))

        @pl.when(inside)
        def _():
            lax.fori_loop(1, NQ // 2, one, 0)

        @pl.when(jnp.logical_not(inside))
        def _():
            lax.fori_loop(0, NQ // 2, one, 0)

    for tile in range(NQ // 2):
        part_s[16 + tile, 0:8, :] = g_out[tile * 8:(tile + 1) * 8]
        part_s[16 + tile, 8:12, :] = g_proj[tile * 4:(tile + 1) * 4]
    scatter(NQ // 2)

    g_mix = jnp.zeros((2 * C, 2 * C), F32)
    g_stem = jnp.zeros((2 * VOX, 2 * C), F32)
    for step in range(ROWS // CHUNK):
        rows = slice(step * CHUNK, (step + 1) * CHUNK)
        shape = (CHUNK // SLOTS, SLOTS, 2 * C)
        d_pre2 = (slope2_s[rows, :].reshape(shape) * d_mixed[None]).reshape(CHUNK, 2 * C).astype(BF16)
        g_mix = g_mix + dot(ht_s[:, rows], d_pre2)
        d_hid = (dot_nt(d_pre2, w_mix2).reshape(shape) + d_spread[None]).reshape(CHUNK, 2 * C)
        d_pre1 = (d_hid * slope1_s[rows, :]).astype(BF16)
        g_stem = g_stem + dot(xt_s[:, rows], d_pre1)
    g_mix = g_mix[:C, :C] + g_mix[C:, C:]
    g_stem = g_stem[:VOX, :C] + g_stem[VOX:, C:]
    for tile in range(NQ // 2):
        part_s[tile, 0:8, :] = g_mix[tile * 8:(tile + 1) * 8]
        part_s[tile, 8:12, :] = g_stem[tile * 4:(tile + 1) * 4]

    scatter(0)
    gath_s[q] = part_s[q]

    out_sum = jnp.zeros((HALF, 1), F32)
    for half in range(2):
        hit = picked[half][SLOTS + HALF:]
        out_sum = out_sum + jnp.sum(jnp.where(hit, sums[half], 0.0), axis=1, keepdims=True)
    affinity = jnp.sum(chosen[SLOTS:SLOTS + HALF] * chosen[SLOTS + HALF:], axis=1, keepdims=True)
    loss = jnp.log(out_sum) - affinity * (1.0 / TEMPERATURE)
    square = iota((HALF, HALF), 0) == iota((HALF, HALF), 1)
    loss_ref[...] = jnp.sum(jnp.where(square, loss, 0.0), axis=0, keepdims=True)

    arrived(gath_s.at[0:NQ - 1], 8)
    zed_s[z] = jnp.sum(gath_s[...], axis=0)
    for step in range(NZ // 2, 0, -1):
        for sign in (1, -1):
            if step < NZ // 2 or sign == 1:
                send(zed_s.at[z], zed_s.at[z], 9, z_peer(sign * step))
    arrived(zed_s.at[0:NZ - 1], 9)
    fin_s[q] = jnp.sum(zed_s[...], axis=0)

    def spread(step, carry):
        send(fin_s.at[q], fin_s.at[q], 10, q_peer(lax.rem(q + step, NQ)))
        return carry

    lax.fori_loop(1, NQ, spread, 0)
    arrived(fin_s.at[0:NQ - 1], 10)

    def normal(g):
        return g * lax.rsqrt(jnp.mean(g * g) + EPS)

    up_ref[0:64] = normal(jnp.concatenate([fin_s[tile, 8:12, :] for tile in range(16)], axis=0))
    up_ref[64:192] = normal(fin_s[0:16, 0:8, :].reshape(C, C))
    up_ref[192:320] = normal(fin_s[16:32, 0:8, :].reshape(C, C))
    up_ref[320:384] = normal(jnp.concatenate([fin_s[16 + tile, 8:12, :] for tile in range(16)], axis=0))

    sent(emb_s.at[0, 0:2 * NEAR], 0)
    sent(cnt_s.at[0, 0:2 * NEAR], 1)
    sent(emb_s.at[0, 0:far], 2)
    sent(cnt_s.at[0, 0:far], 3)
    sent(emb_s.at[0:NP - 1, 0:2 * NEAR + 1], 4)
    sent(emb_s.at[0:NP - 1, 0:far], 5)
    sent(cnt_s.at[0:NP - 1], 6)
    sent(tot_s.at[0:NP - 1], 7)
    sent(gath_s.at[0:NQ - 1], 8)
    sent(zed_s.at[0:NZ - 1], 9)
    sent(fin_s.at[0:NQ - 1], 10)


def store(up_ref, loss_ref, stem_ref, mix_ref, out_ref, proj_ref, out_loss_ref):
    stem_ref[...] = up_ref[0:64]
    mix_ref[...] = up_ref[64:192]
    out_ref[...] = up_ref[192:320]
    proj_ref[...] = up_ref[320:384]
    out_loss_ref[...] = loss_ref[...]


def on_device(cutouts, counts, partner, w_stem, w_mix, w_out, w_proj):
    vmem = pl.BlockSpec(memory_space=pltpu.VMEM)
    hbm = pl.BlockSpec(memory_space=pltpu.HBM)
    updates, loss = pl.pallas_call(
        kernel,
        out_shape=(jax.ShapeDtypeStruct((384, 128), F32), jax.ShapeDtypeStruct((1, HALF), F32)),
        in_specs=[hbm] * 7,
        out_specs=(vmem,) * 2,
        scratch_shapes=[
            pltpu.VMEM((SLOTS, PATCHES * VOX), BF16),
            pltpu.VMEM((1, 1), jnp.int32),
            pltpu.VMEM((1, NODES), jnp.int32),
            pltpu.VMEM((VOX, C), BF16),
            pltpu.VMEM((C, C), BF16),
            pltpu.VMEM((C, C), BF16),
            pltpu.VMEM((E, C), BF16),
            pltpu.SemaphoreType.DMA((7,)),
            pltpu.VMEM((ROWS, 128), BF16),
            pltpu.VMEM((ROWS, 2 * C), BF16),
            pltpu.VMEM((ROWS, 2 * C), F32),
            pltpu.VMEM((ROWS, 2 * C), F32),
            pltpu.VMEM((128, ROWS), BF16),
            pltpu.VMEM((2 * C, ROWS), BF16),
            pltpu.VMEM((NP, NZ, HALF, 128), BF16),
            pltpu.VMEM((NP, NZ, 1, 128), F32),
            pltpu.VMEM((NP, 2, LINE), F32),
            pltpu.VMEM((NQ, 12, 128), F32),
            pltpu.VMEM((NQ, 12, 128), F32),
            pltpu.VMEM((NZ, 12, 128), F32),
            pltpu.VMEM((NQ, 12, 128), F32),
            pltpu.SemaphoreType.DMA((11,)),
            pltpu.SemaphoreType.DMA((11,)),
        ],
        compiler_params=pltpu.CompilerParams(
            collective_id=0, has_side_effects=True, vmem_limit_bytes=56 * 1024 * 1024
        ),
    )(cutouts[0], counts, partner, w_stem, w_mix, w_out, w_proj.T)
    outs = pl.pallas_call(
        store,
        out_shape=(
            jax.ShapeDtypeStruct((VOX, C), F32),
            jax.ShapeDtypeStruct((C, C), F32),
            jax.ShapeDtypeStruct((C, C), F32),
            jax.ShapeDtypeStruct((E, C), F32),
            jax.ShapeDtypeStruct((1, HALF), F32),
        ),
        in_specs=[vmem] * 2,
        out_specs=(vmem,) * 5,
    )(updates, loss)
    return outs[:3] + (outs[3].T, outs[4][None])


def solution(mesh):
    in_specs = (P("rep", "vol", None), P("rep", "vol"), P("rep", None), P(), P(), P(), P())
    out_specs = (P(), P(), P(), P(), P("rep", "vol", None))
    return jax.shard_map(
        on_device, mesh=mesh, in_specs=in_specs, out_specs=out_specs, check_vma=False
    )
```

```python
import functools

import jax
import jax.numpy as jnp
from jax import lax
from jax.experimental import pallas as pl
from jax.experimental.pallas import tpu as pltpu
from jax.sharding import PartitionSpec as P

MESH = pl.DeviceIdType.MESH
F32 = jnp.float32
BF16 = jnp.bfloat16
HIGHEST = lax.Precision.HIGHEST

NZ, NP, NY = 16, 8, 4
NV = NZ * NP
NQ = NP * NY
C, E, VOX, PATCHES = 128, 64, 64, 64
SLOTS, HALF = 32, 16
NODES = 2048
DEAD = NV * SLOTS - NODES
NEAR = 4
PAIRS = PATCHES // 2
ROWS = PAIRS * SLOTS
CHUNK = 256
LINE = NZ * HALF
TEMPERATURE = 0.2
LOG2E = 1.4426950408889634
SCALE = LOG2E / TEMPERATURE
EPS = 1e-6
(LINE_NEAR_A, LINE_NEAR_B, LINE_FAR_A, LINE_FAR_B, PLANE_NEAR_A, PLANE_NEAR_B, PLANE_FAR_A, PLANE_FAR_B,
 COUNT_NEAR, COUNT_FAR, PLANE_COUNT, TOTAL, PIECE, PIECE_Z, RESULT) = range(15)
KINDS = 15


def iota(shape, dim):
    return lax.broadcasted_iota(jnp.int32, shape, dim)


def dot(a, b, precision=None):
    return lax.dot_general(a, b, (((1,), (0,)), ((), ())), precision=precision, preferred_element_type=F32)


def dot_nt(a, b):
    return lax.dot_general(a, b, (((1,), (1,)), ((), ())), preferred_element_type=F32)


def dot_tn(a, b):
    return lax.dot_general(a, b, (((0,), (0,)), ((), ())), preferred_element_type=F32)


def sigmoid(v):
    return 1.0 / (1.0 + jnp.exp(-v))


def twice(v):
    return jnp.concatenate([v, v], axis=1)


def fold(v):
    half = v.shape[1] // 2
    return v[:, :half] + v[:, half:]


def block_diagonal(w):
    zero = jnp.zeros_like(w)
    return jnp.concatenate(
        [jnp.concatenate([w, zero], axis=1), jnp.concatenate([zero, w], axis=1)], axis=0
    )


def kernel(
    cut_hbm, count_hbm, partner_hbm, stem_hbm, mix_hbm, out_hbm, proj_hbm,
    up_ref, loss_ref,
    cut_ref, count_ref, partner_ref, stem_ref, mix_ref, out_ref, proj_ref, load_sem,
    x_s, hid_s, slope1_s, slope2_s, xt_s, ht_s,
    emb_s, cnt_s, tot_s, part_s, gath_s, zed_s, fin_s,
    send_sem, recv_sem,
):
    vol = lax.axis_index("vol")
    rep = lax.axis_index("rep")
    z = vol // NP
    p = lax.rem(vol, NP)
    q = rep * NP + p

    def z_peer(step):
        return (lax.rem(z + step + NZ, NZ) * NP + p, rep)

    def p_peer(step):
        return (z * NP + lax.rem(p + step, NP), rep)

    def q_peer(other):
        return (z * NP + lax.rem(other, NP), other // NP)

    def send(src, dst, kind, device):
        pltpu.make_async_remote_copy(
            src_ref=src, dst_ref=dst, send_sem=send_sem.at[kind], recv_sem=recv_sem.at[kind],
            device_id=device, device_id_type=MESH,
        ).start()

    def arrived(ref, kind):
        pltpu.make_async_copy(ref, ref, recv_sem.at[kind]).wait()

    def sent(ref, kind):
        pltpu.make_async_copy(ref, ref, send_sem.at[kind]).wait()

    loads = [
        pltpu.make_async_copy(source, target, load_sem.at[number])
        for number, (source, target) in enumerate([
            (cut_hbm, cut_ref), (stem_hbm, stem_ref), (mix_hbm, mix_ref), (count_hbm, count_ref),
            (out_hbm, out_ref), (proj_hbm, proj_ref), (partner_hbm, partner_ref),
        ])
    ]
    for load in loads:
        load.start()

    barrier = pltpu.get_barrier_semaphore()
    greeted = 0
    for step in range(NEAR, 0, -1):
        for sign in (1, -1):
            pl.semaphore_signal(barrier, inc=1, device_id=z_peer(sign * step), device_id_type=MESH)
            greeted += 1
    for step in range(1, NY):
        pl.semaphore_signal(
            barrier, inc=1, device_id=(vol, lax.rem(rep + step, NY)), device_id_type=MESH
        )
        greeted += 1
    for step in range(1, NP):
        pl.semaphore_signal(barrier, inc=1, device_id=p_peer(step), device_id_type=MESH)
        greeted += 1

    for load in loads:
        load.wait()
    count = count_ref[...]
    cnt_s[p, NEAR] = jnp.broadcast_to(count, (1, 128)).astype(F32)
    w_stem2 = block_diagonal(stem_ref[...])
    w_mix2 = block_diagonal(mix_ref[...])
    for pair in range(PAIRS):
        x_s[pair * SLOTS:(pair + 1) * SLOTS, :] = cut_ref[:, pair * 128:(pair + 1) * 128]

    def forward(step, sums):
        hid_sum, mix_sum = sums
        rows = pl.ds(pl.multiple_of(step * CHUNK, CHUNK), CHUNK)
        pre1 = dot(x_s[rows, :], w_stem2)
        sig1 = sigmoid(pre1)
        hidden = (pre1 * sig1).astype(BF16)
        slope1_s[rows, :] = sig1 * (1.0 + pre1 * (1.0 - sig1))
        hid_s[rows, :] = hidden
        pre2 = dot(hidden, w_mix2)
        sig2 = sigmoid(pre2)
        mixed = (pre2 * sig2).astype(BF16)
        slope2_s[rows, :] = sig2 * (1.0 + pre2 * (1.0 - sig2))
        hid_sum = hid_sum + jnp.sum(hidden.astype(F32).reshape(CHUNK // SLOTS, SLOTS, 2 * C), axis=0)
        mix_sum = mix_sum + jnp.sum(mixed.astype(F32).reshape(CHUNK // SLOTS, SLOTS, 2 * C), axis=0)
        return hid_sum, mix_sum

    start = jnp.zeros((SLOTS, 2 * C), F32)
    hid_sum, mix_sum = lax.fori_loop(0, ROWS // CHUNK, forward, (start, start))
    hid_sum, mix_sum = fold(hid_sum), fold(mix_sum)
    w_out = out_ref[...]
    pooled = ((hid_sum + dot(mix_sum, w_out.astype(F32), HIGHEST)) * (1.0 / PATCHES)).astype(BF16)
    raw = dot_nt(pooled, proj_ref[...])
    inv_norm = lax.rsqrt(jnp.sum(raw * raw, axis=1, keepdims=True) + EPS)
    unit = raw * inv_norm
    live = iota((SLOTS, E), 0) < count
    embed = jnp.where(live, unit, 0.0).astype(BF16)
    emb_s[p, NEAR] = jnp.concatenate([embed[:HALF], embed[HALF:]], axis=1)

    pl.semaphore_wait(barrier, greeted)

    own = emb_s.at[p, NEAR]
    own_count = cnt_s.at[p, NEAR]
    for step in range(NEAR, 0, -1):
        for sign in (1, -1):
            send(own, emb_s.at[p, NEAR - sign * step], LINE_NEAR_B if step > 2 else LINE_NEAR_A, z_peer(sign * step))
    for step in range(NEAR, 0, -1):
        for sign in (1, -1):
            send(own_count, cnt_s.at[p, NEAR - sign * step], COUNT_NEAR, z_peer(sign * step))

    def share(first, last, kind):
        block = emb_s.at[p, first:last]
        for step in range(1, NP):
            send(block, block, kind, p_peer(step))

    def relay(source, target, blocks, kind, towards, ref=emb_s):
        send(ref.at[p, source:source + blocks], ref.at[p, target:target + blocks], kind, z_peer(towards))

    xt_s[...] = x_s[...].T
    ht_s[...] = hid_s[...].T
    terms, rest = [], mix_sum
    for _ in range(3):
        terms.append(rest.astype(BF16))
        rest = rest - terms[-1].astype(F32)
    mix_terms = jnp.concatenate(terms, axis=0).T
    zero_slots = jnp.zeros((SLOTS, E), BF16)
    anchors = jnp.concatenate(
        [jnp.concatenate([embed, zero_slots], axis=1), jnp.concatenate([zero_slots, embed], axis=1)], axis=0
    )

    arrived(emb_s.at[0, 0:4], LINE_NEAR_A)
    relay(5, 9, 2, LINE_FAR_A, -NEAR)
    relay(2, 14, 2, LINE_FAR_A, NEAR)
    share(2, 7, PLANE_NEAR_A)
    arrived(emb_s.at[0, 0:4], LINE_NEAR_B)
    relay(7, 11, 2, LINE_FAR_B, -NEAR)
    relay(1, 13, 1, LINE_FAR_B, NEAR)
    share(0, 2, PLANE_NEAR_B)
    share(7, 9, PLANE_NEAR_B)
    arrived(cnt_s.at[0, 0:8], COUNT_NEAR)
    relay(5, 9, 4, COUNT_FAR, -NEAR, cnt_s)
    relay(1, 13, 3, COUNT_FAR, NEAR, cnt_s)
    arrived(emb_s.at[0, 0:4], LINE_FAR_A)
    share(9, 11, PLANE_FAR_A)
    share(14, 16, PLANE_FAR_A)
    arrived(emb_s.at[0, 0:3], LINE_FAR_B)
    share(11, 14, PLANE_FAR_B)
    arrived(cnt_s.at[0, 0:7], COUNT_FAR)
    count_block = cnt_s.at[p]
    for step in range(1, NP):
        send(count_block, count_block, PLANE_COUNT, p_peer(step))

    line = emb_s[p].reshape(LINE, 128)
    low = iota((LINE, 128), 1) < E
    turned = jnp.concatenate([line[:, E:], line[:, :E]], axis=1)
    none = jnp.zeros_like(line)
    columns = jnp.concatenate(
        [
            jnp.where(low, line, none), jnp.where(low, turned, none),
            jnp.where(low, none, turned), jnp.where(low, none, line),
        ],
        axis=0,
    )

    def powers(block, against):
        return jnp.exp2(dot_nt(block, against) * SCALE)

    def add_rows(total, first, last):
        block = emb_s[:, first:last].reshape(NP * (last - first) * HALF, 128)
        e = powers(block, columns)
        return total + jnp.sum(e.reshape(e.shape[0] // 8, 8, 4 * LINE), axis=0)

    diagonal = iota((LINE, LINE), 0) == iota((LINE, LINE), 1)
    self_sum = jnp.concatenate(
        [
            jnp.sum(jnp.where(diagonal, powers(line, columns[at:at + LINE]), 0.0), axis=0, keepdims=True)
            for at in (0, 3 * LINE)
        ],
        axis=1,
    )
    total = jnp.zeros((8, 4 * LINE), F32)
    arrived(emb_s.at[0:NP - 1, 0:5], PLANE_NEAR_A)
    total = add_rows(total, 2, 7)
    arrived(emb_s.at[0:NP - 1, 0:4], PLANE_NEAR_B)
    total = add_rows(add_rows(total, 0, 2), 7, 9)
    arrived(emb_s.at[0:NP - 1, 0:4], PLANE_FAR_A)
    total = add_rows(add_rows(total, 9, 11), 14, 16)
    arrived(emb_s.at[0:NP - 1, 0:3], PLANE_FAR_B)
    total = add_rows(total, 11, 14)
    line_sum = fold(jnp.sum(total, axis=0, keepdims=True)) - float(DEAD) - self_sum
    tot_s[p] = jnp.concatenate([line_sum[:, :LINE], line_sum[:, LINE:]], axis=0)
    own_total = tot_s.at[p]
    for step in range(1, NP):
        send(own_total, own_total, TOTAL, p_peer(step))

    every = emb_s[...].reshape(NP * LINE, 128)
    wide = NP * LINE
    exps = jnp.exp2(dot_nt(anchors, every) * SCALE)
    row = iota((2 * SLOTS, wide), 0)
    col = iota((2 * SLOTS, wide), 1)
    slot = lax.rem(row, SLOTS)
    self_score = (row // SLOTS == slot // HALF) & (col == p * LINE + NEAR * HALF + lax.rem(slot, HALF))
    exps = jnp.where(self_score, 0.0, exps)
    row_sum = jnp.sum(exps, axis=1, keepdims=True)
    own_sum = row_sum[:SLOTS] + row_sum[SLOTS:] - float(DEAD)
    own_inv = 1.0 / own_sum
    row_weight = (exps * jnp.concatenate([own_inv, own_inv], axis=0)).astype(BF16)

    arrived(cnt_s.at[0:NP - 1], PLANE_COUNT)
    counts = cnt_s[...]
    by_plane = jnp.sum(counts, axis=0)

    def place(relative):
        return lax.rem(z + relative + NZ - NEAR, NZ)

    plane_row = place(iota((NZ, 1, 128), 0))
    numbers = [[], []]
    own_offset = jnp.sum(jnp.where(plane_row < z, by_plane, 0.0), axis=0)
    before = [own_offset]
    for group in range(2):
        relative = iota((NZ, 1, 128), 2) // HALF + group * (NZ // 2)
        offset = jnp.sum(jnp.where(plane_row < place(relative), by_plane, 0.0), axis=0)
        inside = lax.rem(iota((1, 128), 1), HALF).astype(F32)
        for part in range(NP):
            amount = jnp.sum(jnp.where(iota((NZ, 1, 128), 0) == relative, counts[part], 0.0), axis=0)
            for half in range(2):
                position = inside + float(half * HALF)
                numbers[half].append((part, group, jnp.where(position < amount, offset + position, -1.0)))
            offset = offset + amount
    for part in range(NP):
        own_offset = own_offset + jnp.where(part < p, counts[part, NEAR], 0.0)
    number = []
    for half in range(2):
        ordered = sorted(numbers[half], key=lambda item: item[:2])
        number.append(jnp.concatenate([value for _, _, value in ordered], axis=1))

    table = partner_ref[...].astype(F32)
    node = iota((1, NODES), 1).astype(F32)
    own_number = own_offset[:, :1] + iota((SLOTS, 1), 0).astype(F32)
    out_number = (iota((HALF, 1), 0) * NV + vol).astype(F32)
    wanted = jnp.concatenate([own_number, out_number], axis=0)
    mates = jnp.sum(jnp.where(node == wanted, table, 0.0), axis=1, keepdims=True)
    pick = jnp.concatenate([mates, out_number], axis=0)
    picked = [(number[half] == pick) for half in range(2)]
    ones = [jnp.where(match, 1.0, 0.0).astype(BF16) for match in picked]
    first = dot(jnp.concatenate([row_weight] + ones, axis=0), every)
    rows_term = first[:SLOTS, :E] + first[SLOTS:2 * SLOTS, E:]
    n_pick = SLOTS + 2 * HALF
    chosen = first[2 * SLOTS:2 * SLOTS + n_pick, :E] + first[2 * SLOTS + n_pick:, E:]
    companion = chosen[:SLOTS]

    arrived(tot_s.at[0:NP - 1], TOTAL)
    sums = [
        jnp.concatenate([tot_s[part, half:half + 1, :] for part in range(NP)], axis=1) for half in range(2)
    ]
    col_weight = jnp.concatenate(
        [exps[half * SLOTS:(half + 1) * SLOTS] * (1.0 / sums[half]) for half in range(2)], axis=0
    ).astype(BF16)
    second = dot(col_weight, every)
    cols_term = second[:SLOTS, :E] + second[SLOTS:, E:]

    d_embed = (rows_term + cols_term - 2.0 * companion) * (1.0 / TEMPERATURE)
    radial = jnp.sum(unit * d_embed, axis=1, keepdims=True)
    d_raw = jnp.where(live, inv_norm * (d_embed - unit * radial), 0.0).astype(BF16)
    g_proj = dot_tn(d_raw, pooled)
    d_sum = (dot(d_raw, proj_ref[...]) * (1.0 / PATCHES)).astype(BF16)
    d_sum32 = d_sum.astype(F32)
    g_out = dot(mix_terms, jnp.concatenate([d_sum] * 3, axis=0))
    d_mixed = twice(dot_nt(d_sum, w_out))
    d_spread = twice(d_sum32)

    def scatter(first):
        def one(step, carry):
            to = first + lax.rem(q + step, NQ // 2)
            send(part_s.at[to], gath_s.at[q], PIECE, q_peer(to))
            return carry

        inside = (q // (NQ // 2) == first // (NQ // 2))

        @pl.when(inside)
        def _():
            lax.fori_loop(1, NQ // 2, one, 0)

        @pl.when(jnp.logical_not(inside))
        def _():
            lax.fori_loop(0, NQ // 2, one, 0)

    for tile in range(NQ // 2):
        part_s[16 + tile, 0:8, :] = g_out[tile * 8:(tile + 1) * 8]
        part_s[16 + tile, 8:12, :] = g_proj[tile * 4:(tile + 1) * 4]
    scatter(NQ // 2)

    g_mix = jnp.zeros((2 * C, 2 * C), F32)
    g_stem = jnp.zeros((2 * VOX, 2 * C), F32)
    for step in range(ROWS // CHUNK):
        rows = slice(step * CHUNK, (step + 1) * CHUNK)
        shape = (CHUNK // SLOTS, SLOTS, 2 * C)
        d_pre2 = (slope2_s[rows, :].reshape(shape) * d_mixed[None]).reshape(CHUNK, 2 * C).astype(BF16)
        g_mix = g_mix + dot(ht_s[:, rows], d_pre2)
        d_hid = (dot_nt(d_pre2, w_mix2).reshape(shape) + d_spread[None]).reshape(CHUNK, 2 * C)
        d_pre1 = (d_hid * slope1_s[rows, :]).astype(BF16)
        g_stem = g_stem + dot(xt_s[:, rows], d_pre1)
    g_mix = g_mix[:C, :C] + g_mix[C:, C:]
    g_stem = g_stem[:VOX, :C] + g_stem[VOX:, C:]
    for tile in range(NQ // 2):
        part_s[tile, 0:8, :] = g_mix[tile * 8:(tile + 1) * 8]
        part_s[tile, 8:12, :] = g_stem[tile * 4:(tile + 1) * 4]

    scatter(0)
    gath_s[q] = part_s[q]

    out_sum = jnp.zeros((HALF, 1), F32)
    for half in range(2):
        hit = picked[half][SLOTS + HALF:]
        out_sum = out_sum + jnp.sum(jnp.where(hit, sums[half], 0.0), axis=1, keepdims=True)
    affinity = jnp.sum(chosen[SLOTS:SLOTS + HALF] * chosen[SLOTS + HALF:], axis=1, keepdims=True)
    loss = jnp.log(out_sum) - affinity * (1.0 / TEMPERATURE)
    square = iota((HALF, HALF), 0) == iota((HALF, HALF), 1)
    loss_ref[...] = jnp.sum(jnp.where(square, loss, 0.0), axis=0, keepdims=True)

    arrived(gath_s.at[0:NQ - 1], PIECE)
    zed_s[z] = jnp.sum(gath_s[...], axis=0)
    for step in range(NZ // 2, 0, -1):
        for sign in (1, -1):
            if step < NZ // 2 or sign == 1:
                send(zed_s.at[z], zed_s.at[z], PIECE_Z, z_peer(sign * step))
    arrived(zed_s.at[0:NZ - 1], PIECE_Z)
    fin_s[q] = jnp.sum(zed_s[...], axis=0)

    def spread(step, carry):
        send(fin_s.at[q], fin_s.at[q], RESULT, q_peer(lax.rem(q + step, NQ)))
        return carry

    lax.fori_loop(1, NQ, spread, 0)
    arrived(fin_s.at[0:NQ - 1], RESULT)

    def normal(g):
        return g * lax.rsqrt(jnp.mean(g * g) + EPS)

    up_ref[0:64] = normal(jnp.concatenate([fin_s[tile, 8:12, :] for tile in range(16)], axis=0))
    up_ref[64:192] = normal(fin_s[0:16, 0:8, :].reshape(C, C))
    up_ref[192:320] = normal(fin_s[16:32, 0:8, :].reshape(C, C))
    up_ref[320:384] = normal(jnp.concatenate([fin_s[16 + tile, 8:12, :] for tile in range(16)], axis=0))

    for kind, ref in [
        (LINE_NEAR_A, emb_s.at[0, 0:4]), (LINE_NEAR_B, emb_s.at[0, 0:4]), (COUNT_NEAR, cnt_s.at[0, 0:8]),
        (LINE_FAR_A, emb_s.at[0, 0:4]), (LINE_FAR_B, emb_s.at[0, 0:3]), (COUNT_FAR, cnt_s.at[0, 0:7]),
        (PLANE_NEAR_A, emb_s.at[0:NP - 1, 0:5]), (PLANE_NEAR_B, emb_s.at[0:NP - 1, 0:4]),
        (PLANE_FAR_A, emb_s.at[0:NP - 1, 0:4]), (PLANE_FAR_B, emb_s.at[0:NP - 1, 0:3]),
        (PLANE_COUNT, cnt_s.at[0:NP - 1]), (TOTAL, tot_s.at[0:NP - 1]), (PIECE, gath_s.at[0:NQ - 1]),
        (PIECE_Z, zed_s.at[0:NZ - 1]), (RESULT, fin_s.at[0:NQ - 1]),
    ]:
        sent(ref, kind)


def store(up_ref, loss_ref, stem_ref, mix_ref, out_ref, proj_ref, out_loss_ref):
    stem_ref[...] = up_ref[0:64]
    mix_ref[...] = up_ref[64:192]
    out_ref[...] = up_ref[192:320]
    proj_ref[...] = up_ref[320:384]
    out_loss_ref[...] = loss_ref[...]


def on_device(cutouts, counts, partner, w_stem, w_mix, w_out, w_proj):
    vmem = pl.BlockSpec(memory_space=pltpu.VMEM)
    hbm = pl.BlockSpec(memory_space=pltpu.HBM)
    updates, loss = pl.pallas_call(
        kernel,
        out_shape=(jax.ShapeDtypeStruct((384, 128), F32), jax.ShapeDtypeStruct((1, HALF), F32)),
        in_specs=[hbm] * 7,
        out_specs=(vmem,) * 2,
        scratch_shapes=[
            pltpu.VMEM((SLOTS, PATCHES * VOX), BF16),
            pltpu.VMEM((1, 1), jnp.int32),
            pltpu.VMEM((1, NODES), jnp.int32),
            pltpu.VMEM((VOX, C), BF16),
            pltpu.VMEM((C, C), BF16),
            pltpu.VMEM((C, C), BF16),
            pltpu.VMEM((E, C), BF16),
            pltpu.SemaphoreType.DMA((7,)),
            pltpu.VMEM((ROWS, 128), BF16),
            pltpu.VMEM((ROWS, 2 * C), BF16),
            pltpu.VMEM((ROWS, 2 * C), F32),
            pltpu.VMEM((ROWS, 2 * C), F32),
            pltpu.VMEM((128, ROWS), BF16),
            pltpu.VMEM((2 * C, ROWS), BF16),
            pltpu.VMEM((NP, NZ, HALF, 128), BF16),
            pltpu.VMEM((NP, NZ, 1, 128), F32),
            pltpu.VMEM((NP, 2, LINE), F32),
            pltpu.VMEM((NQ, 12, 128), F32),
            pltpu.VMEM((NQ, 12, 128), F32),
            pltpu.VMEM((NZ, 12, 128), F32),
            pltpu.VMEM((NQ, 12, 128), F32),
            pltpu.SemaphoreType.DMA((KINDS,)),
            pltpu.SemaphoreType.DMA((KINDS,)),
        ],
        compiler_params=pltpu.CompilerParams(
            collective_id=0, has_side_effects=True, vmem_limit_bytes=56 * 1024 * 1024
        ),
    )(cutouts[0], counts, partner, w_stem, w_mix, w_out, w_proj.T)
    outs = pl.pallas_call(
        store,
        out_shape=(
            jax.ShapeDtypeStruct((VOX, C), F32),
            jax.ShapeDtypeStruct((C, C), F32),
            jax.ShapeDtypeStruct((C, C), F32),
            jax.ShapeDtypeStruct((E, C), F32),
            jax.ShapeDtypeStruct((1, HALF), F32),
        ),
        in_specs=[vmem] * 2,
        out_specs=(vmem,) * 5,
    )(updates, loss)
    return outs[:3] + (outs[3].T, outs[4][None])


def solution(mesh):
    in_specs = (P("rep", "vol", None), P("rep", "vol"), P("rep", None), P(), P(), P(), P())
    out_specs = (P(), P(), P(), P(), P("rep", "vol", None))
    return jax.shard_map(
        on_device, mesh=mesh, in_specs=in_specs, out_specs=out_specs, check_vma=False
    )
```

```python
import functools

import jax
import jax.numpy as jnp
from jax import lax
from jax.experimental import pallas as pl
from jax.experimental.pallas import tpu as pltpu
from jax.sharding import PartitionSpec as P

MESH = pl.DeviceIdType.MESH
F32 = jnp.float32
BF16 = jnp.bfloat16

NZ, NP, NY = 16, 8, 4
NV = NZ * NP
NQ = NP * NY
C, E, VOX, PATCHES = 128, 64, 64, 64
SLOTS, HALF = 32, 16
NODES = 2048
DEAD = NV * SLOTS - NODES
NEAR = 4
PAIRS = PATCHES // 2
ROWS = PAIRS * SLOTS
CHUNK = 256
LINE = NZ * HALF
TEMPERATURE = 0.2
LOG2E = 1.4426950408889634
SCALE = LOG2E / TEMPERATURE
EPS = 1e-6
(LINE_NEAR_A, LINE_NEAR_B, LINE_FAR_A, LINE_FAR_B, PLANE_NEAR_A, PLANE_NEAR_B, PLANE_FAR_A, PLANE_FAR_B,
 COUNT_NEAR, COUNT_FAR, PLANE_COUNT, TOTAL, PIECE, PIECE_Z, RESULT) = range(15)
KINDS = 15


def iota(shape, dim):
    return lax.broadcasted_iota(jnp.int32, shape, dim)


def dot(a, b):
    return lax.dot_general(a, b, (((1,), (0,)), ((), ())), preferred_element_type=F32)


def dot_nt(a, b):
    return lax.dot_general(a, b, (((1,), (1,)), ((), ())), preferred_element_type=F32)


def dot_tn(a, b):
    return lax.dot_general(a, b, (((0,), (0,)), ((), ())), preferred_element_type=F32)


def sigmoid(v):
    d = 1.0 + jnp.exp(jnp.minimum(-v, 80.0))
    r = pl.reciprocal(d, approx=True)
    r = r * (2.0 - d * r)
    return r * (2.0 - d * r)


def exact_terms(v):
    terms = []
    for _ in range(3):
        terms.append(v.astype(BF16))
        v = v - terms[-1].astype(F32)
    return jnp.concatenate(terms, axis=0)


def twice(v):
    return jnp.concatenate([v, v], axis=1)


def fold(v):
    half = v.shape[1] // 2
    return v[:, :half] + v[:, half:]


def block_diagonal(w):
    zero = jnp.zeros_like(w)
    return jnp.concatenate(
        [jnp.concatenate([w, zero], axis=1), jnp.concatenate([zero, w], axis=1)], axis=0
    )


def kernel(
    cut_hbm, count_hbm, partner_hbm, stem_hbm, mix_hbm, out_hbm, proj_hbm,
    up_ref, loss_ref,
    cut_ref, count_ref, partner_ref, stem_ref, mix_ref, out_ref, proj_ref, load_sem,
    x_s, hid_s, slope1_s, slope2_s, xt_s, ht_s,
    emb_s, cnt_s, tot_s, part_s, gath_s, zed_s, fin_s,
    send_sem, recv_sem,
):
    vol = lax.axis_index("vol")
    rep = lax.axis_index("rep")
    z = vol // NP
    p = lax.rem(vol, NP)
    x, core = p // 2, lax.rem(p, 2)
    xs = [lax.rem(x + step, 4) for step in range(4)]
    ys = [lax.rem(rep + step, 4) for step in range(4)]
    mate = 1 - core
    piece = core * (NQ // 2) + rep * 4 + x
    plane = [z * NP + xs[dx] * 2 for dx in range(4)]
    p_peers = [plane[dx] + to for dx in (2, 1, 3) for to in (core, mate)] + [plane[0] + mate]
    apart = sorted(
        [(dy, dx) for dy in range(4) for dx in range(4) if (dy, dx) != (0, 0)],
        key=lambda step: -min(step[0], 4 - step[0]) - min(step[1], 4 - step[1]),
    )

    def z_peer(step):
        return (lax.rem(z + step + NZ, NZ) * NP + p, rep)

    def send(src, dst, kind, device):
        pltpu.make_async_remote_copy(
            src_ref=src, dst_ref=dst, send_sem=send_sem.at[kind], recv_sem=recv_sem.at[kind],
            device_id=device, device_id_type=MESH,
        ).start()

    def arrived(ref, kind):
        pltpu.make_async_copy(ref, ref, recv_sem.at[kind]).wait()

    def sent(ref, kind):
        pltpu.make_async_copy(ref, ref, send_sem.at[kind]).wait()

    loads = [
        pltpu.make_async_copy(source, target, load_sem.at[number])
        for number, (source, target) in enumerate([
            (stem_hbm, stem_ref), (cut_hbm, cut_ref), (mix_hbm, mix_ref), (count_hbm, count_ref),
            (out_hbm, out_ref), (proj_hbm, proj_ref), (partner_hbm, partner_ref),
        ])
    ]
    for load in loads:
        load.start()

    barrier = pltpu.get_barrier_semaphore()
    greeted = 0
    for step in range(NEAR, 0, -1):
        for sign in (1, -1):
            pl.semaphore_signal(barrier, inc=1, device_id=z_peer(sign * step), device_id_type=MESH)
            greeted += 1
    for step in range(1, NY):
        pl.semaphore_signal(
            barrier, inc=1, device_id=(vol, ys[step]), device_id_type=MESH
        )
        greeted += 1
    for peer in p_peers:
        pl.semaphore_signal(barrier, inc=1, device_id=(peer, rep), device_id_type=MESH)
        greeted += 1

    loads[0].wait()
    w_stem2 = block_diagonal(stem_ref[...])
    loads[1].wait()
    loads[2].wait()
    w_mix2 = block_diagonal(mix_ref[...])
    hid_sum = mix_sum = jnp.zeros((SLOTS, 2 * C), F32)
    tall = (CHUNK // SLOTS, SLOTS, 2 * C)
    for first in range(0, ROWS, CHUNK):
        for pair in range(first // SLOTS, (first + CHUNK) // SLOTS):
            x_s[pair * SLOTS:(pair + 1) * SLOTS, :] = cut_ref[:, pair * 128:(pair + 1) * 128]
        rows = slice(first, first + CHUNK)
        pre1 = dot(x_s[rows, :], w_stem2)
        hidden = (pre1 * sigmoid(pre1)).astype(BF16)
        hid_s[rows, :] = hidden
        pre2 = dot(hidden, w_mix2)
        mixed = (pre2 * sigmoid(pre2)).astype(BF16)
        hid_sum = hid_sum + jnp.sum(hidden.astype(F32).reshape(tall), axis=0)
        mix_sum = mix_sum + jnp.sum(mixed.astype(F32).reshape(tall), axis=0)
    hid_sum, mix_sum = fold(hid_sum), fold(mix_sum)
    for load in loads[3:]:
        load.wait()
    count = count_ref[...]
    cnt_s[p, NEAR] = jnp.broadcast_to(count, (1, 128)).astype(F32)
    w_out = out_ref[...]
    mix_terms = exact_terms(mix_sum)
    branch = dot(mix_terms, w_out)
    branch = branch[:SLOTS] + branch[SLOTS:2 * SLOTS] + branch[2 * SLOTS:]
    pooled = ((hid_sum + branch) * (1.0 / PATCHES)).astype(BF16)
    raw = dot_nt(pooled, proj_ref[...])
    inv_norm = lax.rsqrt(jnp.sum(raw * raw, axis=1, keepdims=True) + EPS)
    unit = raw * inv_norm
    live = iota((SLOTS, E), 0) < count
    embed = jnp.where(live, unit, 0.0).astype(BF16)
    emb_s[p, NEAR] = jnp.concatenate([embed[:HALF], embed[HALF:]], axis=1)

    pl.semaphore_wait(barrier, greeted)

    own = emb_s.at[p, NEAR]
    own_count = cnt_s.at[p, NEAR]
    for step in range(NEAR, 0, -1):
        for sign in (1, -1):
            send(own, emb_s.at[p, NEAR - sign * step], LINE_NEAR_B if step > 2 else LINE_NEAR_A, z_peer(sign * step))
    for step in range(NEAR, 0, -1):
        for sign in (1, -1):
            send(own_count, cnt_s.at[p, NEAR - sign * step], COUNT_NEAR, z_peer(sign * step))

    def share(first, last, kind):
        block = emb_s.at[p, first:last]
        for peer in p_peers:
            send(block, block, kind, (peer, rep))

    def relay(source, target, blocks, kind, towards, ref=emb_s):
        send(ref.at[p, source:source + blocks], ref.at[p, target:target + blocks], kind, z_peer(towards))

    arrived(emb_s.at[0, 0:4], LINE_NEAR_A)
    relay(5, 9, 2, LINE_FAR_A, -NEAR)
    relay(2, 14, 2, LINE_FAR_A, NEAR)
    share(2, 7, PLANE_NEAR_A)
    arrived(emb_s.at[0, 0:4], LINE_NEAR_B)
    relay(7, 11, 2, LINE_FAR_B, -NEAR)
    relay(1, 13, 1, LINE_FAR_B, NEAR)
    share(0, 2, PLANE_NEAR_B)
    share(7, 9, PLANE_NEAR_B)
    arrived(cnt_s.at[0, 0:8], COUNT_NEAR)
    relay(5, 9, 4, COUNT_FAR, -NEAR, cnt_s)
    relay(1, 13, 3, COUNT_FAR, NEAR, cnt_s)

    def slopes(step, carry):
        rows = pl.ds(pl.multiple_of(step * CHUNK, CHUNK), CHUNK)
        pre1 = dot(x_s[rows, :], w_stem2)
        sig1 = sigmoid(pre1)
        slope1_s[rows, :] = sig1 * (1.0 + pre1 * (1.0 - sig1))
        pre2 = dot(hid_s[rows, :], w_mix2)
        sig2 = sigmoid(pre2)
        slope2_s[rows, :] = sig2 * (1.0 + pre2 * (1.0 - sig2))
        return carry

    lax.fori_loop(0, ROWS // CHUNK, slopes, 0)
    xt_s[...] = x_s[...].T
    ht_s[...] = hid_s[...].T
    mix_turned = mix_terms.T
    zero_slots = jnp.zeros((SLOTS, E), BF16)
    anchors = jnp.concatenate(
        [jnp.concatenate([embed, zero_slots], axis=1), jnp.concatenate([zero_slots, embed], axis=1)], axis=0
    )

    arrived(emb_s.at[0, 0:4], LINE_FAR_A)
    share(9, 11, PLANE_FAR_A)
    share(14, 16, PLANE_FAR_A)
    arrived(emb_s.at[0, 0:3], LINE_FAR_B)
    share(11, 14, PLANE_FAR_B)
    arrived(cnt_s.at[0, 0:7], COUNT_FAR)
    count_block = cnt_s.at[p]
    for peer in p_peers:
        send(count_block, count_block, PLANE_COUNT, (peer, rep))

    line = emb_s[p].reshape(LINE, 128)
    low = iota((LINE, 128), 1) < E
    turned = jnp.concatenate([line[:, E:], line[:, :E]], axis=1)
    none = jnp.zeros_like(line)
    columns = jnp.concatenate(
        [
            jnp.where(low, line, none), jnp.where(low, turned, none),
            jnp.where(low, none, turned), jnp.where(low, none, line),
        ],
        axis=0,
    )

    def powers(block, against):
        return jnp.exp2(dot_nt(block, against) * SCALE)

    def add_rows(total, first, last):
        block = emb_s[:, first:last].reshape(NP * (last - first) * HALF, 128)
        e = powers(block, columns)
        return total + jnp.sum(e.reshape(e.shape[0] // 8, 8, 4 * LINE), axis=0)

    diagonal = iota((LINE, LINE), 0) == iota((LINE, LINE), 1)
    self_sum = jnp.concatenate(
        [
            jnp.sum(jnp.where(diagonal, powers(line, columns[at:at + LINE]), 0.0), axis=0, keepdims=True)
            for at in (0, 3 * LINE)
        ],
        axis=1,
    )
    total = jnp.zeros((8, 4 * LINE), F32)
    arrived(emb_s.at[0:NP - 1, 0:5], PLANE_NEAR_A)
    total = add_rows(total, 2, 7)
    arrived(emb_s.at[0:NP - 1, 0:4], PLANE_NEAR_B)
    total = add_rows(add_rows(total, 0, 2), 7, 9)
    arrived(emb_s.at[0:NP - 1, 0:4], PLANE_FAR_A)
    total = add_rows(add_rows(total, 9, 11), 14, 16)
    arrived(emb_s.at[0:NP - 1, 0:3], PLANE_FAR_B)
    total = add_rows(total, 11, 14)
    line_sum = fold(jnp.sum(total, axis=0, keepdims=True)) - float(DEAD) - self_sum
    tot_s[p] = jnp.concatenate([line_sum[:, :LINE], line_sum[:, LINE:]], axis=0)
    own_total = tot_s.at[p]
    for peer in p_peers:
        send(own_total, own_total, TOTAL, (peer, rep))

    every = emb_s[...].reshape(NP * LINE, 128)
    wide = NP * LINE
    exps = jnp.exp2(dot_nt(anchors, every) * SCALE)
    row = iota((2 * SLOTS, wide), 0)
    col = iota((2 * SLOTS, wide), 1)
    slot = lax.rem(row, SLOTS)
    self_score = (row // SLOTS == slot // HALF) & (col == p * LINE + NEAR * HALF + lax.rem(slot, HALF))
    exps = jnp.where(self_score, 0.0, exps)
    row_sum = jnp.sum(exps, axis=1, keepdims=True)
    own_sum = row_sum[:SLOTS] + row_sum[SLOTS:] - float(DEAD)
    own_inv = 1.0 / own_sum
    row_weight = (exps * jnp.concatenate([own_inv, own_inv], axis=0)).astype(BF16)

    arrived(cnt_s.at[0:NP - 1], PLANE_COUNT)
    counts = cnt_s[...]
    by_plane = jnp.sum(counts, axis=0)

    def place(relative):
        return lax.rem(z + relative + NZ - NEAR, NZ)

    plane_row = place(iota((NZ, 1, 128), 0))
    numbers = [[], []]
    own_offset = jnp.sum(jnp.where(plane_row < z, by_plane, 0.0), axis=0)
    before = [own_offset]
    for group in range(2):
        relative = iota((NZ, 1, 128), 2) // HALF + group * (NZ // 2)
        offset = jnp.sum(jnp.where(plane_row < place(relative), by_plane, 0.0), axis=0)
        inside = lax.rem(iota((1, 128), 1), HALF).astype(F32)
        for part in range(NP):
            amount = jnp.sum(jnp.where(iota((NZ, 1, 128), 0) == relative, counts[part], 0.0), axis=0)
            for half in range(2):
                position = inside + float(half * HALF)
                numbers[half].append((part, group, jnp.where(position < amount, offset + position, -1.0)))
            offset = offset + amount
    for part in range(NP):
        own_offset = own_offset + jnp.where(part < p, counts[part, NEAR], 0.0)
    number = []
    for half in range(2):
        ordered = sorted(numbers[half], key=lambda item: item[:2])
        number.append(jnp.concatenate([value for _, _, value in ordered], axis=1))

    table = partner_ref[...].astype(F32)
    node = iota((1, NODES), 1).astype(F32)
    own_number = own_offset[:, :1] + iota((SLOTS, 1), 0).astype(F32)
    out_number = (iota((HALF, 1), 0) * NV + vol).astype(F32)
    wanted = jnp.concatenate([own_number, out_number], axis=0)
    mates = jnp.sum(jnp.where(node == wanted, table, 0.0), axis=1, keepdims=True)
    pick = jnp.concatenate([mates, out_number], axis=0)
    picked = [(number[half] == pick) for half in range(2)]
    ones = [jnp.where(match, 1.0, 0.0).astype(BF16) for match in picked]
    first = dot(jnp.concatenate([row_weight] + ones, axis=0), every)
    rows_term = first[:SLOTS, :E] + first[SLOTS:2 * SLOTS, E:]
    n_pick = SLOTS + 2 * HALF
    chosen = first[2 * SLOTS:2 * SLOTS + n_pick, :E] + first[2 * SLOTS + n_pick:, E:]
    companion = chosen[:SLOTS]

    arrived(tot_s.at[0:NP - 1], TOTAL)
    sums = [
        jnp.concatenate([tot_s[part, half:half + 1, :] for part in range(NP)], axis=1) for half in range(2)
    ]
    col_weight = jnp.concatenate(
        [exps[half * SLOTS:(half + 1) * SLOTS] * (1.0 / sums[half]) for half in range(2)], axis=0
    ).astype(BF16)
    second = dot(col_weight, every)
    cols_term = second[:SLOTS, :E] + second[SLOTS:, E:]

    d_embed = (rows_term + cols_term - 2.0 * companion) * (1.0 / TEMPERATURE)
    radial = jnp.sum(unit * d_embed, axis=1, keepdims=True)
    d_raw = jnp.where(live, inv_norm * (d_embed - unit * radial), 0.0).astype(BF16)
    g_proj = dot_tn(d_raw, pooled)
    d_sum = (dot(d_raw, proj_ref[...]) * (1.0 / PATCHES)).astype(BF16)
    d_sum32 = d_sum.astype(F32)
    g_out = dot(mix_turned, jnp.concatenate([d_sum] * 3, axis=0))
    d_mixed = twice(dot_nt(d_sum, w_out))
    d_spread = twice(d_sum32)

    def scatter(to):
        for dy, dx in apart:
            at = to * (NQ // 2) + ys[dy] * 4 + xs[dx]
            send(part_s.at[at], gath_s.at[piece], PIECE, (plane[dx] + to, ys[dy]))

        @pl.when(core != to)
        def _():
            at = to * (NQ // 2) + rep * 4 + x
            send(part_s.at[at], gath_s.at[piece], PIECE, (plane[0] + to, rep))

    for tile in range(NQ // 2):
        part_s[16 + tile, 0:8, :] = g_out[tile * 8:(tile + 1) * 8]
        part_s[16 + tile, 8:12, :] = g_proj[tile * 4:(tile + 1) * 4]
    scatter(1)

    g_mix = jnp.zeros((2 * C, 2 * C), F32)
    g_stem = jnp.zeros((2 * VOX, 2 * C), F32)
    for step in range(ROWS // CHUNK):
        rows = slice(step * CHUNK, (step + 1) * CHUNK)
        shape = (CHUNK // SLOTS, SLOTS, 2 * C)
        d_pre2 = (slope2_s[rows, :].reshape(shape) * d_mixed[None]).reshape(CHUNK, 2 * C).astype(BF16)
        g_mix = g_mix + dot(ht_s[:, rows], d_pre2)
        d_hid = (dot_nt(d_pre2, w_mix2).reshape(shape) + d_spread[None]).reshape(CHUNK, 2 * C)
        d_pre1 = (d_hid * slope1_s[rows, :]).astype(BF16)
        g_stem = g_stem + dot(xt_s[:, rows], d_pre1)
    g_mix = g_mix[:C, :C] + g_mix[C:, C:]
    g_stem = g_stem[:VOX, :C] + g_stem[VOX:, C:]
    for tile in range(NQ // 2):
        part_s[tile, 0:8, :] = g_mix[tile * 8:(tile + 1) * 8]
        part_s[tile, 8:12, :] = g_stem[tile * 4:(tile + 1) * 4]

    scatter(0)
    gath_s[piece] = part_s[piece]

    out_sum = jnp.zeros((HALF, 1), F32)
    for half in range(2):
        hit = picked[half][SLOTS + HALF:]
        out_sum = out_sum + jnp.sum(jnp.where(hit, sums[half], 0.0), axis=1, keepdims=True)
    affinity = jnp.sum(chosen[SLOTS:SLOTS + HALF] * chosen[SLOTS + HALF:], axis=1, keepdims=True)
    loss = jnp.log(out_sum) - affinity * (1.0 / TEMPERATURE)
    square = iota((HALF, HALF), 0) == iota((HALF, HALF), 1)
    loss_ref[...] = jnp.sum(jnp.where(square, loss, 0.0), axis=0, keepdims=True)

    arrived(gath_s.at[0:NQ - 1], PIECE)
    zed_s[z] = jnp.sum(gath_s[...], axis=0)
    for step in range(NZ // 2, 0, -1):
        for sign in (1, -1):
            if step < NZ // 2 or sign == 1:
                send(zed_s.at[z], zed_s.at[z], PIECE_Z, z_peer(sign * step))
    arrived(zed_s.at[0:NZ - 1], PIECE_Z)
    fin_s[piece] = jnp.sum(zed_s[...], axis=0)

    result = fin_s.at[piece]
    for dy, dx in apart:
        for to in range(2):
            send(result, result, RESULT, (plane[dx] + to, ys[dy]))
    send(result, result, RESULT, (plane[0] + mate, rep))
    arrived(fin_s.at[0:NQ - 1], RESULT)

    def normal(g):
        return g * lax.rsqrt(jnp.mean(g * g) + EPS)

    up_ref[0:64] = normal(jnp.concatenate([fin_s[tile, 8:12, :] for tile in range(16)], axis=0))
    up_ref[64:192] = normal(fin_s[0:16, 0:8, :].reshape(C, C))
    up_ref[192:320] = normal(fin_s[16:32, 0:8, :].reshape(C, C))
    up_ref[320:384] = normal(jnp.concatenate([fin_s[16 + tile, 8:12, :] for tile in range(16)], axis=0))

    for kind, ref in [
        (LINE_NEAR_A, emb_s.at[0, 0:4]), (LINE_NEAR_B, emb_s.at[0, 0:4]), (COUNT_NEAR, cnt_s.at[0, 0:8]),
        (LINE_FAR_A, emb_s.at[0, 0:4]), (LINE_FAR_B, emb_s.at[0, 0:3]), (COUNT_FAR, cnt_s.at[0, 0:7]),
        (PLANE_NEAR_A, emb_s.at[0:NP - 1, 0:5]), (PLANE_NEAR_B, emb_s.at[0:NP - 1, 0:4]),
        (PLANE_FAR_A, emb_s.at[0:NP - 1, 0:4]), (PLANE_FAR_B, emb_s.at[0:NP - 1, 0:3]),
        (PLANE_COUNT, cnt_s.at[0:NP - 1]), (TOTAL, tot_s.at[0:NP - 1]), (PIECE, gath_s.at[0:NQ - 1]),
        (PIECE_Z, zed_s.at[0:NZ - 1]), (RESULT, fin_s.at[0:NQ - 1]),
    ]:
        sent(ref, kind)


def store(up_ref, loss_ref, stem_ref, mix_ref, out_ref, proj_ref, out_loss_ref):
    stem_ref[...] = up_ref[0:64]
    mix_ref[...] = up_ref[64:192]
    out_ref[...] = up_ref[192:320]
    proj_ref[...] = up_ref[320:384]
    out_loss_ref[...] = loss_ref[...]


def on_device(cutouts, counts, partner, w_stem, w_mix, w_out, w_proj):
    vmem = pl.BlockSpec(memory_space=pltpu.VMEM)
    hbm = pl.BlockSpec(memory_space=pltpu.HBM)
    updates, loss = pl.pallas_call(
        kernel,
        out_shape=(jax.ShapeDtypeStruct((384, 128), F32), jax.ShapeDtypeStruct((1, HALF), F32)),
        in_specs=[hbm] * 7,
        out_specs=(vmem,) * 2,
        scratch_shapes=[
            pltpu.VMEM((SLOTS, PATCHES * VOX), BF16),
            pltpu.VMEM((1, 1), jnp.int32),
            pltpu.VMEM((1, NODES), jnp.int32),
            pltpu.VMEM((VOX, C), BF16),
            pltpu.VMEM((C, C), BF16),
            pltpu.VMEM((C, C), BF16),
            pltpu.VMEM((E, C), BF16),
            pltpu.SemaphoreType.DMA((7,)),
            pltpu.VMEM((ROWS, 128), BF16),
            pltpu.VMEM((ROWS, 2 * C), BF16),
            pltpu.VMEM((ROWS, 2 * C), F32),
            pltpu.VMEM((ROWS, 2 * C), F32),
            pltpu.VMEM((128, ROWS), BF16),
            pltpu.VMEM((2 * C, ROWS), BF16),
            pltpu.VMEM((NP, NZ, HALF, 128), BF16),
            pltpu.VMEM((NP, NZ, 1, 128), F32),
            pltpu.VMEM((NP, 2, LINE), F32),
            pltpu.VMEM((NQ, 12, 128), F32),
            pltpu.VMEM((NQ, 12, 128), F32),
            pltpu.VMEM((NZ, 12, 128), F32),
            pltpu.VMEM((NQ, 12, 128), F32),
            pltpu.SemaphoreType.DMA((KINDS,)),
            pltpu.SemaphoreType.DMA((KINDS,)),
        ],
        compiler_params=pltpu.CompilerParams(
            collective_id=0, has_side_effects=True, vmem_limit_bytes=56 * 1024 * 1024
        ),
    )(cutouts[0], counts, partner, w_stem, w_mix, w_out, w_proj.T)
    outs = pl.pallas_call(
        store,
        out_shape=(
            jax.ShapeDtypeStruct((VOX, C), F32),
            jax.ShapeDtypeStruct((C, C), F32),
            jax.ShapeDtypeStruct((C, C), F32),
            jax.ShapeDtypeStruct((E, C), F32),
            jax.ShapeDtypeStruct((1, HALF), F32),
        ),
        in_specs=[vmem] * 2,
        out_specs=(vmem,) * 5,
    )(updates, loss)
    return outs[:3] + (outs[3].T, outs[4][None])


def solution(mesh):
    in_specs = (P("rep", "vol", None), P("rep", "vol"), P("rep", None), P(), P(), P(), P())
    out_specs = (P(), P(), P(), P(), P("rep", "vol", None))
    return jax.shard_map(
        on_device, mesh=mesh, in_specs=in_specs, out_specs=out_specs, check_vma=False
    )
```

```python
import functools

import jax
import jax.numpy as jnp
from jax import lax
from jax.experimental import pallas as pl
from jax.experimental.pallas import tpu as pltpu
from jax.sharding import PartitionSpec as P

MESH = pl.DeviceIdType.MESH
F32 = jnp.float32
BF16 = jnp.bfloat16

NZ, NP, NY = 16, 8, 4
NV = NZ * NP
NQ = NP * NY
C, E, VOX, PATCHES = 128, 64, 64, 64
SLOTS, HALF = 32, 16
NODES = 2048
DEAD = NV * SLOTS - NODES
NEAR = 4
PAIRS = PATCHES // 2
ROWS = PAIRS * SLOTS
CHUNK = 256
LINE = NZ * HALF
TEMPERATURE = 0.2
LOG2E = 1.4426950408889634
SCALE = LOG2E / TEMPERATURE
EPS = 1e-6
(LINE_NEAR_A, LINE_NEAR_B, LINE_FAR_A, LINE_FAR_B, PLANE_NEAR_A, PLANE_NEAR_B, PLANE_FAR_A, PLANE_FAR_B,
 COUNT_NEAR, COUNT_FAR, PLANE_COUNT, TOTAL, PIECE, PIECE_Z, RESULT) = range(15)
KINDS = 15


def iota(shape, dim):
    return lax.broadcasted_iota(jnp.int32, shape, dim)


def dot(a, b):
    return lax.dot_general(a, b, (((1,), (0,)), ((), ())), preferred_element_type=F32)


def dot_nt(a, b):
    return lax.dot_general(a, b, (((1,), (1,)), ((), ())), preferred_element_type=F32)


def dot_tn(a, b):
    return lax.dot_general(a, b, (((0,), (0,)), ((), ())), preferred_element_type=F32)


def sigmoid(v):
    d = 1.0 + jnp.exp(jnp.minimum(-v, 80.0))
    r = pl.reciprocal(d, approx=True)
    r = r * (2.0 - d * r)
    return r * (2.0 - d * r)


def exact_terms(v):
    terms = []
    for _ in range(3):
        terms.append(v.astype(BF16))
        v = v - terms[-1].astype(F32)
    return jnp.concatenate(terms, axis=0)


def twice(v):
    return jnp.concatenate([v, v], axis=1)


def fold(v):
    half = v.shape[1] // 2
    return v[:, :half] + v[:, half:]


def block_diagonal(w):
    zero = jnp.zeros_like(w)
    return jnp.concatenate(
        [jnp.concatenate([w, zero], axis=1), jnp.concatenate([zero, w], axis=1)], axis=0
    )


def kernel(
    cut_hbm, count_hbm, partner_hbm, stem_hbm, mix_hbm, out_hbm, proj_hbm,
    up_ref, loss_ref,
    cut_ref, count_ref, partner_ref, stem_ref, mix_ref, out_ref, proj_ref, load_sem,
    x_s, hid_s, slope1_s, slope2_s, xt_s, ht_s,
    emb_s, cnt_s, tot_s, part_s, gath_s, zed_s, fin_s,
    send_sem, recv_sem,
):
    vol = lax.axis_index("vol")
    rep = lax.axis_index("rep")
    z = vol // NP
    p = lax.rem(vol, NP)
    x, core = p // 2, lax.rem(p, 2)
    xs = [lax.rem(x + step, 4) for step in range(4)]
    ys = [lax.rem(rep + step, 4) for step in range(4)]
    mate = 1 - core
    piece = core * (NQ // 2) + rep * 4 + x
    plane = [z * NP + xs[dx] * 2 for dx in range(4)]
    p_peers = [plane[dx] + to for dx in (2, 1, 3) for to in (core, mate)] + [plane[0] + mate]
    apart = sorted(
        [(dy, dx) for dy in range(4) for dx in range(4) if (dy, dx) != (0, 0)],
        key=lambda step: -min(step[0], 4 - step[0]) - min(step[1], 4 - step[1]),
    )

    def z_peer(step):
        return (lax.rem(z + step + NZ, NZ) * NP + p, rep)

    def send(src, dst, kind, device):
        pltpu.make_async_remote_copy(
            src_ref=src, dst_ref=dst, send_sem=send_sem.at[kind], recv_sem=recv_sem.at[kind],
            device_id=device, device_id_type=MESH,
        ).start()

    def arrived(ref, kind):
        pltpu.make_async_copy(ref, ref, recv_sem.at[kind]).wait()

    def sent(ref, kind):
        pltpu.make_async_copy(ref, ref, send_sem.at[kind]).wait()

    loads = [
        pltpu.make_async_copy(source, target, load_sem.at[number])
        for number, (source, target) in enumerate([
            (stem_hbm, stem_ref), (cut_hbm, cut_ref), (mix_hbm, mix_ref), (count_hbm, count_ref),
            (out_hbm, out_ref), (proj_hbm, proj_ref), (partner_hbm, partner_ref),
        ])
    ]
    for load in loads:
        load.start()

    barrier = pltpu.get_barrier_semaphore()
    greeted = 0
    for step in range(NEAR, 0, -1):
        for sign in (1, -1):
            pl.semaphore_signal(barrier, inc=1, device_id=z_peer(sign * step), device_id_type=MESH)
            greeted += 1
    for step in range(1, NY):
        pl.semaphore_signal(
            barrier, inc=1, device_id=(vol, ys[step]), device_id_type=MESH
        )
        greeted += 1
    for peer in p_peers:
        pl.semaphore_signal(barrier, inc=1, device_id=(peer, rep), device_id_type=MESH)
        greeted += 1

    loads[0].wait()
    w_stem2 = block_diagonal(stem_ref[...])
    loads[1].wait()
    loads[2].wait()
    w_mix2 = block_diagonal(mix_ref[...])
    hid_sum = mix_sum = jnp.zeros((SLOTS, 2 * C), F32)
    tall = (CHUNK // SLOTS, SLOTS, 2 * C)
    for first in range(0, ROWS, CHUNK):
        for pair in range(first // SLOTS, (first + CHUNK) // SLOTS):
            x_s[pair * SLOTS:(pair + 1) * SLOTS, :] = cut_ref[:, pair * 128:(pair + 1) * 128]
        rows = slice(first, first + CHUNK)
        pre1 = dot(x_s[rows, :], w_stem2)
        hidden = (pre1 * sigmoid(pre1)).astype(BF16)
        hid_s[rows, :] = hidden
        pre2 = dot(hidden, w_mix2)
        mixed = (pre2 * sigmoid(pre2)).astype(BF16)
        hid_sum = hid_sum + jnp.sum(hidden.astype(F32).reshape(tall), axis=0)
        mix_sum = mix_sum + jnp.sum(mixed.astype(F32).reshape(tall), axis=0)
    hid_sum, mix_sum = fold(hid_sum), fold(mix_sum)
    for load in loads[3:]:
        load.wait()
    count = count_ref[...]
    cnt_s[p, NEAR] = jnp.broadcast_to(count, (1, 128)).astype(F32)
    w_out = out_ref[...]
    mix_terms = exact_terms(mix_sum)
    branch = dot(mix_terms, w_out)
    branch = branch[:SLOTS] + branch[SLOTS:2 * SLOTS] + branch[2 * SLOTS:]
    pooled = ((hid_sum + branch) * (1.0 / PATCHES)).astype(BF16)
    raw = dot_nt(pooled, proj_ref[...])
    inv_norm = lax.rsqrt(jnp.sum(raw * raw, axis=1, keepdims=True) + EPS)
    unit = raw * inv_norm
    live = iota((SLOTS, E), 0) < count
    embed = jnp.where(live, unit, 0.0).astype(BF16)
    emb_s[p, NEAR] = jnp.concatenate([embed[:HALF], embed[HALF:]], axis=1)

    pl.semaphore_wait(barrier, greeted)

    own = emb_s.at[p, NEAR]
    own_count = cnt_s.at[p, NEAR]
    for step in range(NEAR, 0, -1):
        for sign in (1, -1):
            send(own, emb_s.at[p, NEAR - sign * step], LINE_NEAR_B if step > 2 else LINE_NEAR_A, z_peer(sign * step))
    for step in range(NEAR, 0, -1):
        for sign in (1, -1):
            send(own_count, cnt_s.at[p, NEAR - sign * step], COUNT_NEAR, z_peer(sign * step))

    def share(first, last, kind):
        block = emb_s.at[p, first:last]
        for peer in p_peers:
            send(block, block, kind, (peer, rep))

    def relay(source, target, blocks, kind, towards, ref=emb_s):
        send(ref.at[p, source:source + blocks], ref.at[p, target:target + blocks], kind, z_peer(towards))

    arrived(emb_s.at[0, 0:4], LINE_NEAR_A)
    relay(5, 9, 2, LINE_FAR_A, -NEAR)
    relay(2, 14, 2, LINE_FAR_A, NEAR)
    share(2, 7, PLANE_NEAR_A)
    arrived(emb_s.at[0, 0:4], LINE_NEAR_B)
    relay(7, 11, 2, LINE_FAR_B, -NEAR)
    relay(1, 13, 1, LINE_FAR_B, NEAR)
    share(0, 2, PLANE_NEAR_B)
    share(7, 9, PLANE_NEAR_B)
    arrived(cnt_s.at[0, 0:8], COUNT_NEAR)
    relay(5, 9, 4, COUNT_FAR, -NEAR, cnt_s)
    relay(1, 13, 3, COUNT_FAR, NEAR, cnt_s)

    def slopes(step, carry):
        rows = pl.ds(pl.multiple_of(step * CHUNK, CHUNK), CHUNK)
        pre1 = dot(x_s[rows, :], w_stem2)
        sig1 = sigmoid(pre1)
        slope1_s[rows, :] = sig1 * (1.0 + pre1 * (1.0 - sig1))
        pre2 = dot(hid_s[rows, :], w_mix2)
        sig2 = sigmoid(pre2)
        slope2_s[rows, :] = sig2 * (1.0 + pre2 * (1.0 - sig2))
        return carry

    lax.fori_loop(0, ROWS // CHUNK, slopes, 0)
    xt_s[...] = x_s[...].T
    ht_s[...] = hid_s[...].T
    mix_turned = mix_terms.T
    zero_slots = jnp.zeros((SLOTS, E), BF16)
    anchors = jnp.concatenate(
        [jnp.concatenate([embed, zero_slots], axis=1), jnp.concatenate([zero_slots, embed], axis=1)], axis=0
    )

    arrived(emb_s.at[0, 0:4], LINE_FAR_A)
    share(9, 11, PLANE_FAR_A)
    share(14, 16, PLANE_FAR_A)
    arrived(emb_s.at[0, 0:3], LINE_FAR_B)
    share(11, 14, PLANE_FAR_B)
    arrived(cnt_s.at[0, 0:7], COUNT_FAR)
    count_block = cnt_s.at[p]
    for peer in p_peers:
        send(count_block, count_block, PLANE_COUNT, (peer, rep))

    line = emb_s[p].reshape(LINE, 128)
    low = iota((LINE, 128), 1) < E
    turned = jnp.concatenate([line[:, E:], line[:, :E]], axis=1)
    none = jnp.zeros_like(line)
    columns = jnp.concatenate(
        [
            jnp.where(low, line, none), jnp.where(low, turned, none),
            jnp.where(low, none, turned), jnp.where(low, none, line),
        ],
        axis=0,
    )

    def powers(block, against):
        return jnp.exp2(dot_nt(block, against) * SCALE)

    def add_rows(total, first, last):
        block = emb_s[:, first:last].reshape(NP * (last - first) * HALF, 128)
        e = powers(block, columns)
        return total + jnp.sum(e.reshape(e.shape[0] // 8, 8, 4 * LINE), axis=0)

    diagonal = iota((LINE, LINE), 0) == iota((LINE, LINE), 1)
    self_sum = jnp.concatenate(
        [
            jnp.sum(jnp.where(diagonal, powers(line, columns[at:at + LINE]), 0.0), axis=0, keepdims=True)
            for at in (0, 3 * LINE)
        ],
        axis=1,
    )
    total = jnp.zeros((8, 4 * LINE), F32)
    arrived(emb_s.at[0:NP - 1, 0:5], PLANE_NEAR_A)
    total = add_rows(total, 2, 7)
    arrived(emb_s.at[0:NP - 1, 0:4], PLANE_NEAR_B)
    total = add_rows(add_rows(total, 0, 2), 7, 9)
    arrived(emb_s.at[0:NP - 1, 0:4], PLANE_FAR_A)
    total = add_rows(add_rows(total, 9, 11), 14, 16)
    arrived(emb_s.at[0:NP - 1, 0:3], PLANE_FAR_B)
    total = add_rows(total, 11, 14)
    line_sum = fold(jnp.sum(total, axis=0, keepdims=True)) - float(DEAD) - self_sum
    tot_s[p] = jnp.concatenate([line_sum[:, :LINE], line_sum[:, LINE:]], axis=0)
    own_total = tot_s.at[p]
    for peer in p_peers:
        send(own_total, own_total, TOTAL, (peer, rep))

    every = emb_s[...].reshape(NP * LINE, 128)
    wide = NP * LINE
    exps = jnp.exp2(dot_nt(anchors, every) * SCALE)
    row = iota((2 * SLOTS, wide), 0)
    col = iota((2 * SLOTS, wide), 1)
    slot = lax.rem(row, SLOTS)
    self_score = (row // SLOTS == slot // HALF) & (col == p * LINE + NEAR * HALF + lax.rem(slot, HALF))
    exps = jnp.where(self_score, 0.0, exps)
    row_sum = jnp.sum(exps, axis=1, keepdims=True)
    own_sum = row_sum[:SLOTS] + row_sum[SLOTS:] - float(DEAD)
    own_inv = 1.0 / own_sum
    row_weight = (exps * jnp.concatenate([own_inv, own_inv], axis=0)).astype(BF16)

    arrived(cnt_s.at[0:NP - 1], PLANE_COUNT)
    counts = cnt_s[...]
    by_plane = jnp.sum(counts, axis=0)

    def place(relative):
        return lax.rem(z + relative + NZ - NEAR, NZ)

    plane_row = place(iota((NZ, 1, 128), 0))
    numbers = [[], []]
    own_offset = jnp.sum(jnp.where(plane_row < z, by_plane, 0.0), axis=0)
    before = [own_offset]
    for group in range(2):
        relative = iota((NZ, 1, 128), 2) // HALF + group * (NZ // 2)
        offset = jnp.sum(jnp.where(plane_row < place(relative), by_plane, 0.0), axis=0)
        inside = lax.rem(iota((1, 128), 1), HALF).astype(F32)
        for part in range(NP):
            amount = jnp.sum(jnp.where(iota((NZ, 1, 128), 0) == relative, counts[part], 0.0), axis=0)
            for half in range(2):
                position = inside + float(half * HALF)
                numbers[half].append((part, group, jnp.where(position < amount, offset + position, -1.0)))
            offset = offset + amount
    for part in range(NP):
        own_offset = own_offset + jnp.where(part < p, counts[part, NEAR], 0.0)
    number = []
    for half in range(2):
        ordered = sorted(numbers[half], key=lambda item: item[:2])
        number.append(jnp.concatenate([value for _, _, value in ordered], axis=1))

    table = partner_ref[...].astype(F32)
    node = iota((1, NODES), 1).astype(F32)
    own_number = own_offset[:, :1] + iota((SLOTS, 1), 0).astype(F32)
    out_number = (iota((HALF, 1), 0) * NV + vol).astype(F32)
    wanted = jnp.concatenate([own_number, out_number], axis=0)
    mates = jnp.sum(jnp.where(node == wanted, table, 0.0), axis=1, keepdims=True)
    pick = jnp.concatenate([mates, out_number], axis=0)
    picked = [(number[half] == pick) for half in range(2)]
    ones = [jnp.where(match, 1.0, 0.0).astype(BF16) for match in picked]
    first = dot(jnp.concatenate([row_weight] + ones, axis=0), every)
    rows_term = first[:SLOTS, :E] + first[SLOTS:2 * SLOTS, E:]
    n_pick = SLOTS + 2 * HALF
    chosen = first[2 * SLOTS:2 * SLOTS + n_pick, :E] + first[2 * SLOTS + n_pick:, E:]
    companion = chosen[:SLOTS]

    arrived(tot_s.at[0:NP - 1], TOTAL)
    sums = [
        jnp.concatenate([tot_s[part, half:half + 1, :] for part in range(NP)], axis=1) for half in range(2)
    ]
    col_weight = jnp.concatenate(
        [exps[half * SLOTS:(half + 1) * SLOTS] * (1.0 / sums[half]) for half in range(2)], axis=0
    ).astype(BF16)
    second = dot(col_weight, every)
    cols_term = second[:SLOTS, :E] + second[SLOTS:, E:]

    d_embed = (rows_term + cols_term - 2.0 * companion) * (1.0 / TEMPERATURE)
    radial = jnp.sum(unit * d_embed, axis=1, keepdims=True)
    d_raw = jnp.where(live, inv_norm * (d_embed - unit * radial), 0.0).astype(BF16)
    g_proj = dot_tn(d_raw, pooled)
    d_sum = (dot(d_raw, proj_ref[...]) * (1.0 / PATCHES)).astype(BF16)
    d_sum32 = d_sum.astype(F32)
    g_out = dot(mix_turned, jnp.concatenate([d_sum] * 3, axis=0))
    d_mixed = twice(dot_nt(d_sum, w_out))
    d_spread = twice(d_sum32)

    def scatter(to):
        for dy, dx in apart:
            at = to * (NQ // 2) + ys[dy] * 4 + xs[dx]
            send(part_s.at[at], gath_s.at[piece], PIECE, (plane[dx] + to, ys[dy]))

        @pl.when(core != to)
        def _():
            at = to * (NQ // 2) + rep * 4 + x
            send(part_s.at[at], gath_s.at[piece], PIECE, (plane[0] + to, rep))

    for tile in range(NQ // 2):
        part_s[16 + tile, 0:8, :] = g_out[tile * 8:(tile + 1) * 8]
        part_s[16 + tile, 8:12, :] = g_proj[tile * 4:(tile + 1) * 4]
    scatter(1)

    g_mix = jnp.zeros((2 * C, 2 * C), F32)
    g_stem = jnp.zeros((2 * VOX, 2 * C), F32)
    for step in range(ROWS // CHUNK):
        rows = slice(step * CHUNK, (step + 1) * CHUNK)
        shape = (CHUNK // SLOTS, SLOTS, 2 * C)
        d_pre2 = (slope2_s[rows, :].reshape(shape) * d_mixed[None]).reshape(CHUNK, 2 * C).astype(BF16)
        g_mix = g_mix + dot(ht_s[:, rows], d_pre2)
        d_hid = (dot_nt(d_pre2, w_mix2).reshape(shape) + d_spread[None]).reshape(CHUNK, 2 * C)
        d_pre1 = (d_hid * slope1_s[rows, :]).astype(BF16)
        g_stem = g_stem + dot(xt_s[:, rows], d_pre1)
    g_mix = g_mix[:C, :C] + g_mix[C:, C:]
    g_stem = g_stem[:VOX, :C] + g_stem[VOX:, C:]
    for tile in range(NQ // 2):
        part_s[tile, 0:8, :] = g_mix[tile * 8:(tile + 1) * 8]
        part_s[tile, 8:12, :] = g_stem[tile * 4:(tile + 1) * 4]

    scatter(0)
    gath_s[piece] = part_s[piece]

    out_sum = jnp.zeros((HALF, 1), F32)
    for half in range(2):
        hit = picked[half][SLOTS + HALF:]
        out_sum = out_sum + jnp.sum(jnp.where(hit, sums[half], 0.0), axis=1, keepdims=True)
    affinity = jnp.sum(chosen[SLOTS:SLOTS + HALF] * chosen[SLOTS + HALF:], axis=1, keepdims=True)
    loss = jnp.log(out_sum) - affinity * (1.0 / TEMPERATURE)
    square = iota((HALF, HALF), 0) == iota((HALF, HALF), 1)
    loss_ref[...] = jnp.sum(jnp.where(square, loss, 0.0), axis=0, keepdims=True)

    arrived(gath_s.at[0:NQ - 1], PIECE)
    zed_s[z] = jnp.sum(gath_s[...], axis=0)
    for step in range(NZ // 2, 0, -1):
        for sign in (1, -1):
            if step < NZ // 2 or sign == 1:
                send(zed_s.at[z], zed_s.at[z], PIECE_Z, z_peer(sign * step))
    arrived(zed_s.at[0:NZ - 1], PIECE_Z)
    fin_s[piece] = jnp.sum(zed_s[...], axis=0)

    result = fin_s.at[piece]
    for dy, dx in apart:
        for to in range(2):
            send(result, result, RESULT, (plane[dx] + to, ys[dy]))
    send(result, result, RESULT, (plane[0] + mate, rep))
    arrived(fin_s.at[0:NQ - 1], RESULT)

    def normal(g):
        return g * lax.rsqrt(jnp.mean(g * g) + EPS)

    up_ref[0:64] = normal(jnp.concatenate([fin_s[tile, 8:12, :] for tile in range(16)], axis=0))
    up_ref[64:192] = normal(fin_s[0:16, 0:8, :].reshape(C, C))
    up_ref[192:320] = normal(fin_s[16:32, 0:8, :].reshape(C, C))
    up_ref[320:384] = normal(jnp.concatenate([fin_s[16 + tile, 8:12, :] for tile in range(16)], axis=0))

    for kind, ref in [
        (LINE_NEAR_A, emb_s.at[0, 0:4]), (LINE_NEAR_B, emb_s.at[0, 0:4]), (COUNT_NEAR, cnt_s.at[0, 0:8]),
        (LINE_FAR_A, emb_s.at[0, 0:4]), (LINE_FAR_B, emb_s.at[0, 0:3]), (COUNT_FAR, cnt_s.at[0, 0:7]),
        (PLANE_NEAR_A, emb_s.at[0:NP - 1, 0:5]), (PLANE_NEAR_B, emb_s.at[0:NP - 1, 0:4]),
        (PLANE_FAR_A, emb_s.at[0:NP - 1, 0:4]), (PLANE_FAR_B, emb_s.at[0:NP - 1, 0:3]),
        (PLANE_COUNT, cnt_s.at[0:NP - 1]), (TOTAL, tot_s.at[0:NP - 1]), (PIECE, gath_s.at[0:NQ - 1]),
        (PIECE_Z, zed_s.at[0:NZ - 1]), (RESULT, fin_s.at[0:NQ - 1]),
    ]:
        sent(ref, kind)


def store(up_ref, loss_ref, stem_hbm, mix_hbm, out_hbm, proj_hbm, loss_hbm, sem):
    copies = [
        pltpu.make_async_copy(source, target, sem.at[number])
        for number, (source, target) in enumerate([
            (up_ref.at[64:192], mix_hbm), (up_ref.at[192:320], out_hbm), (up_ref.at[0:64], stem_hbm),
            (up_ref.at[320:384], proj_hbm), (loss_ref, loss_hbm),
        ])
    ]
    for copy in copies:
        copy.start()
    for copy in copies:
        copy.wait()


def on_device(cutouts, counts, partner, w_stem, w_mix, w_out, w_proj):
    vmem = pl.BlockSpec(memory_space=pltpu.VMEM)
    hbm = pl.BlockSpec(memory_space=pltpu.HBM)
    updates, loss = pl.pallas_call(
        kernel,
        out_shape=(jax.ShapeDtypeStruct((384, 128), F32), jax.ShapeDtypeStruct((1, HALF), F32)),
        in_specs=[hbm] * 7,
        out_specs=(vmem,) * 2,
        scratch_shapes=[
            pltpu.VMEM((SLOTS, PATCHES * VOX), BF16),
            pltpu.VMEM((1, 1), jnp.int32),
            pltpu.VMEM((1, NODES), jnp.int32),
            pltpu.VMEM((VOX, C), BF16),
            pltpu.VMEM((C, C), BF16),
            pltpu.VMEM((C, C), BF16),
            pltpu.VMEM((E, C), BF16),
            pltpu.SemaphoreType.DMA((7,)),
            pltpu.VMEM((ROWS, 128), BF16),
            pltpu.VMEM((ROWS, 2 * C), BF16),
            pltpu.VMEM((ROWS, 2 * C), F32),
            pltpu.VMEM((ROWS, 2 * C), F32),
            pltpu.VMEM((128, ROWS), BF16),
            pltpu.VMEM((2 * C, ROWS), BF16),
            pltpu.VMEM((NP, NZ, HALF, 128), BF16),
            pltpu.VMEM((NP, NZ, 1, 128), F32),
            pltpu.VMEM((NP, 2, LINE), F32),
            pltpu.VMEM((NQ, 12, 128), F32),
            pltpu.VMEM((NQ, 12, 128), F32),
            pltpu.VMEM((NZ, 12, 128), F32),
            pltpu.VMEM((NQ, 12, 128), F32),
            pltpu.SemaphoreType.DMA((KINDS,)),
            pltpu.SemaphoreType.DMA((KINDS,)),
        ],
        compiler_params=pltpu.CompilerParams(
            collective_id=0, has_side_effects=True, vmem_limit_bytes=50000 * 1024
        ),
    )(*[v if v is counts else pltpu.with_memory_space_constraint(v, pltpu.HBM) for v in (cutouts[0], counts, partner, w_stem, w_mix, w_out, w_proj.T)])
    outs = pl.pallas_call(
        store,
        out_shape=(
            jax.ShapeDtypeStruct((VOX, C), F32),
            jax.ShapeDtypeStruct((C, C), F32),
            jax.ShapeDtypeStruct((C, C), F32),
            jax.ShapeDtypeStruct((E, C), F32),
            jax.ShapeDtypeStruct((1, HALF), F32),
        ),
        in_specs=[pl.BlockSpec(memory_space=pl.ANY)] * 2,
        out_specs=(hbm,) * 5,
        scratch_shapes=[pltpu.SemaphoreType.DMA((5,))],
        compiler_params=pltpu.CompilerParams(vmem_limit_bytes=4 * 1024 * 1024),
    )(updates, loss)
    return outs[:3] + (outs[3].T, outs[4][None])


def solution(mesh):
    in_specs = (P("rep", "vol", None), P("rep", "vol"), P("rep", None), P(), P(), P(), P())
    out_specs = (P(), P(), P(), P(), P("rep", "vol", None))
    return jax.shard_map(
        on_device, mesh=mesh, in_specs=in_specs, out_specs=out_specs, check_vma=False
    )
```

```python
import functools

import jax
import jax.numpy as jnp
from jax import lax
from jax.experimental import pallas as pl
from jax.experimental.pallas import tpu as pltpu
from jax.sharding import PartitionSpec as P

MESH = pl.DeviceIdType.MESH
F32 = jnp.float32
BF16 = jnp.bfloat16

NZ, NP, NY = 16, 8, 4
NV = NZ * NP
NQ = NP * NY
C, E, VOX, PATCHES = 128, 64, 64, 64
SLOTS, HALF = 32, 16
NODES = 2048
DEAD = NV * SLOTS - NODES
NEAR = 4
PAIRS = PATCHES // 2
ROWS = PAIRS * SLOTS
CHUNK = 256
LINE = NZ * HALF
TEMPERATURE = 0.2
LOG2E = 1.4426950408889634
SCALE = LOG2E / TEMPERATURE
EPS = 1e-6
(LINE_NEAR_A, LINE_NEAR_B, LINE_FAR_A, LINE_FAR_B, PLANE_NEAR_A, PLANE_NEAR_B, PLANE_FAR_A, PLANE_FAR_B,
 COUNT_NEAR, COUNT_FAR, PLANE_COUNT, TOTAL, PIECE, PIECE_Z, RESULT) = range(15)
KINDS = 15


def iota(shape, dim):
    return lax.broadcasted_iota(jnp.int32, shape, dim)


def dot(a, b):
    return lax.dot_general(a, b, (((1,), (0,)), ((), ())), preferred_element_type=F32)


def dot_nt(a, b):
    return lax.dot_general(a, b, (((1,), (1,)), ((), ())), preferred_element_type=F32)


def dot_tn(a, b):
    return lax.dot_general(a, b, (((0,), (0,)), ((), ())), preferred_element_type=F32)


def sigmoid(v):
    d = 1.0 + jnp.exp2(jnp.minimum(v * -LOG2E, 80.0 * LOG2E))
    r = pl.reciprocal(d, approx=True)
    return r * (2.0 - d * r)


def exact_terms(v):
    terms = []
    for _ in range(3):
        terms.append(v.astype(BF16))
        v = v - terms[-1].astype(F32)
    return jnp.concatenate(terms, axis=0)


def twice(v):
    return jnp.concatenate([v, v], axis=1)


def fold(v):
    half = v.shape[1] // 2
    return v[:, :half] + v[:, half:]


def block_diagonal(w):
    zero = jnp.zeros_like(w)
    return jnp.concatenate(
        [jnp.concatenate([w, zero], axis=1), jnp.concatenate([zero, w], axis=1)], axis=0
    )


def kernel(
    cut_hbm, count_hbm, partner_hbm, stem_hbm, mix_hbm, out_hbm, proj_hbm,
    up_ref, loss_ref,
    cut_ref, count_ref, partner_ref, stem_ref, mix_ref, out_ref, proj_ref, load_sem,
    x_s, hid_s, slope1_s, slope2_s, xt_s, ht_s,
    emb_s, cnt_s, tot_s, part_s, gath_s, zed_s, fin_s,
    send_sem, recv_sem,
):
    vol = lax.axis_index("vol")
    rep = lax.axis_index("rep")
    z = vol // NP
    p = lax.rem(vol, NP)
    x, core = p // 2, lax.rem(p, 2)
    xs = [lax.rem(x + step, 4) for step in range(4)]
    ys = [lax.rem(rep + step, 4) for step in range(4)]
    mate = 1 - core
    piece = core * (NQ // 2) + rep * 4 + x
    plane = [z * NP + xs[dx] * 2 for dx in range(4)]
    p_peers = [plane[dx] + to for dx in (2, 1, 3) for to in (core, mate)] + [plane[0] + mate]
    apart = sorted(
        [(dy, dx) for dy in range(4) for dx in range(4) if (dy, dx) != (0, 0)],
        key=lambda step: -min(step[0], 4 - step[0]) - min(step[1], 4 - step[1]),
    )

    def z_peer(step):
        return (lax.rem(z + step + NZ, NZ) * NP + p, rep)

    def send(src, dst, kind, device):
        pltpu.make_async_remote_copy(
            src_ref=src, dst_ref=dst, send_sem=send_sem.at[kind], recv_sem=recv_sem.at[kind],
            device_id=device, device_id_type=MESH,
        ).start()

    def arrived(ref, kind):
        pltpu.make_async_copy(ref, ref, recv_sem.at[kind]).wait()

    def sent(ref, kind):
        pltpu.make_async_copy(ref, ref, send_sem.at[kind]).wait()

    loads = [
        pltpu.make_async_copy(source, target, load_sem.at[number])
        for number, (source, target) in enumerate([
            (stem_hbm, stem_ref), (cut_hbm, cut_ref), (mix_hbm, mix_ref), (count_hbm, count_ref),
            (out_hbm, out_ref), (proj_hbm, proj_ref), (partner_hbm, partner_ref),
        ])
    ]
    for load in loads:
        load.start()

    barrier = pltpu.get_barrier_semaphore()
    greeted = 0
    for step in range(NEAR, 0, -1):
        for sign in (1, -1):
            pl.semaphore_signal(barrier, inc=1, device_id=z_peer(sign * step), device_id_type=MESH)
            greeted += 1
    for step in range(1, NY):
        pl.semaphore_signal(
            barrier, inc=1, device_id=(vol, ys[step]), device_id_type=MESH
        )
        greeted += 1
    for peer in p_peers:
        pl.semaphore_signal(barrier, inc=1, device_id=(peer, rep), device_id_type=MESH)
        greeted += 1

    loads[0].wait()
    w_stem2 = block_diagonal(stem_ref[...])
    loads[1].wait()
    loads[2].wait()
    w_mix2 = block_diagonal(mix_ref[...])
    hid_sum = mix_sum = jnp.zeros((SLOTS, 2 * C), F32)
    tall = (CHUNK // SLOTS, SLOTS, 2 * C)
    for first in range(0, ROWS, CHUNK):
        for pair in range(first // SLOTS, (first + CHUNK) // SLOTS):
            x_s[pair * SLOTS:(pair + 1) * SLOTS, :] = cut_ref[:, pair * 128:(pair + 1) * 128]
        rows = slice(first, first + CHUNK)
        pre1 = dot(x_s[rows, :], w_stem2)
        hidden = (pre1 * sigmoid(pre1)).astype(BF16)
        hid_s[rows, :] = hidden
        pre2 = dot(hidden, w_mix2)
        mixed = (pre2 * sigmoid(pre2)).astype(BF16)
        hid_sum = hid_sum + jnp.sum(hidden.astype(F32).reshape(tall), axis=0)
        mix_sum = mix_sum + jnp.sum(mixed.astype(F32).reshape(tall), axis=0)
    hid_sum, mix_sum = fold(hid_sum), fold(mix_sum)
    for load in loads[3:]:
        load.wait()
    count = count_ref[...]
    cnt_s[p, NEAR] = jnp.broadcast_to(count, (1, 128)).astype(F32)
    w_out = out_ref[...]
    mix_terms = exact_terms(mix_sum)
    branch = dot(mix_terms, w_out)
    branch = branch[:SLOTS] + branch[SLOTS:2 * SLOTS] + branch[2 * SLOTS:]
    pooled = ((hid_sum + branch) * (1.0 / PATCHES)).astype(BF16)
    raw = dot_nt(pooled, proj_ref[...])
    inv_norm = lax.rsqrt(jnp.sum(raw * raw, axis=1, keepdims=True) + EPS)
    unit = raw * inv_norm
    live = iota((SLOTS, E), 0) < count
    embed = jnp.where(live, unit, 0.0).astype(BF16)
    emb_s[p, NEAR] = jnp.concatenate([embed[:HALF], embed[HALF:]], axis=1)

    pl.semaphore_wait(barrier, greeted)

    own = emb_s.at[p, NEAR]
    own_count = cnt_s.at[p, NEAR]
    for step in range(NEAR, 0, -1):
        for sign in (1, -1):
            send(own, emb_s.at[p, NEAR - sign * step], LINE_NEAR_B if step > 2 else LINE_NEAR_A, z_peer(sign * step))
    for step in range(NEAR, 0, -1):
        for sign in (1, -1):
            send(own_count, cnt_s.at[p, NEAR - sign * step], COUNT_NEAR, z_peer(sign * step))

    def share(first, last, kind):
        block = emb_s.at[p, first:last]
        for peer in p_peers:
            send(block, block, kind, (peer, rep))

    def relay(source, target, blocks, kind, towards, ref=emb_s):
        send(ref.at[p, source:source + blocks], ref.at[p, target:target + blocks], kind, z_peer(towards))

    arrived(emb_s.at[0, 0:4], LINE_NEAR_A)
    relay(5, 9, 2, LINE_FAR_A, -NEAR)
    relay(2, 14, 2, LINE_FAR_A, NEAR)
    share(2, 7, PLANE_NEAR_A)
    arrived(emb_s.at[0, 0:4], LINE_NEAR_B)
    relay(7, 11, 2, LINE_FAR_B, -NEAR)
    relay(1, 13, 1, LINE_FAR_B, NEAR)
    share(0, 2, PLANE_NEAR_B)
    share(7, 9, PLANE_NEAR_B)
    arrived(cnt_s.at[0, 0:8], COUNT_NEAR)
    relay(5, 9, 4, COUNT_FAR, -NEAR, cnt_s)
    relay(1, 13, 3, COUNT_FAR, NEAR, cnt_s)

    def slopes(step, carry):
        rows = pl.ds(pl.multiple_of(step * CHUNK, CHUNK), CHUNK)
        pre1 = dot(x_s[rows, :], w_stem2)
        sig1 = sigmoid(pre1)
        slope1_s[rows, :] = sig1 * (1.0 + pre1 * (1.0 - sig1))
        pre2 = dot(hid_s[rows, :], w_mix2)
        sig2 = sigmoid(pre2)
        slope2_s[rows, :] = sig2 * (1.0 + pre2 * (1.0 - sig2))
        return carry

    lax.fori_loop(0, ROWS // CHUNK, slopes, 0)
    xt_s[...] = x_s[...].T
    ht_s[...] = hid_s[...].T
    mix_turned = mix_terms.T
    zero_slots = jnp.zeros((SLOTS, E), BF16)
    anchors = jnp.concatenate(
        [jnp.concatenate([embed, zero_slots], axis=1), jnp.concatenate([zero_slots, embed], axis=1)], axis=0
    )

    arrived(emb_s.at[0, 0:4], LINE_FAR_A)
    share(9, 11, PLANE_FAR_A)
    share(14, 16, PLANE_FAR_A)
    arrived(emb_s.at[0, 0:3], LINE_FAR_B)
    share(11, 14, PLANE_FAR_B)
    arrived(cnt_s.at[0, 0:7], COUNT_FAR)
    count_block = cnt_s.at[p]
    for peer in p_peers:
        send(count_block, count_block, PLANE_COUNT, (peer, rep))

    line = emb_s[p].reshape(LINE, 128)
    low = iota((LINE, 128), 1) < E
    turned = jnp.concatenate([line[:, E:], line[:, :E]], axis=1)
    none = jnp.zeros_like(line)
    columns = jnp.concatenate(
        [
            jnp.where(low, line, none), jnp.where(low, turned, none),
            jnp.where(low, none, turned), jnp.where(low, none, line),
        ],
        axis=0,
    )

    def powers(block, against):
        return jnp.exp2(dot_nt(block, against) * SCALE)

    def add_rows(total, first, last):
        block = emb_s[:, first:last].reshape(NP * (last - first) * HALF, 128)
        e = powers(block, columns)
        return total + jnp.sum(e.reshape(e.shape[0] // 8, 8, 4 * LINE), axis=0)

    diagonal = iota((LINE, LINE), 0) == iota((LINE, LINE), 1)
    self_sum = jnp.concatenate(
        [
            jnp.sum(jnp.where(diagonal, powers(line, columns[at:at + LINE]), 0.0), axis=0, keepdims=True)
            for at in (0, 3 * LINE)
        ],
        axis=1,
    )
    total = jnp.zeros((8, 4 * LINE), F32)
    arrived(emb_s.at[0:NP - 1, 0:5], PLANE_NEAR_A)
    total = add_rows(total, 2, 7)
    arrived(emb_s.at[0:NP - 1, 0:4], PLANE_NEAR_B)
    total = add_rows(add_rows(total, 0, 2), 7, 9)
    arrived(emb_s.at[0:NP - 1, 0:4], PLANE_FAR_A)
    total = add_rows(add_rows(total, 9, 11), 14, 16)
    arrived(emb_s.at[0:NP - 1, 0:3], PLANE_FAR_B)
    total = add_rows(total, 11, 14)
    line_sum = fold(jnp.sum(total, axis=0, keepdims=True)) - float(DEAD) - self_sum
    tot_s[p] = jnp.concatenate([line_sum[:, :LINE], line_sum[:, LINE:]], axis=0)
    own_total = tot_s.at[p]
    for peer in p_peers:
        send(own_total, own_total, TOTAL, (peer, rep))

    every = emb_s[...].reshape(NP * LINE, 128)
    wide = NP * LINE
    exps = jnp.exp2(dot_nt(anchors, every) * SCALE)
    row = iota((2 * SLOTS, wide), 0)
    col = iota((2 * SLOTS, wide), 1)
    slot = lax.rem(row, SLOTS)
    self_score = (row // SLOTS == slot // HALF) & (col == p * LINE + NEAR * HALF + lax.rem(slot, HALF))
    exps = jnp.where(self_score, 0.0, exps)
    row_sum = jnp.sum(exps, axis=1, keepdims=True)
    own_sum = row_sum[:SLOTS] + row_sum[SLOTS:] - float(DEAD)
    own_inv = 1.0 / own_sum
    row_weight = (exps * jnp.concatenate([own_inv, own_inv], axis=0)).astype(BF16)

    arrived(cnt_s.at[0:NP - 1], PLANE_COUNT)
    counts = cnt_s[...]
    by_plane = jnp.sum(counts, axis=0)

    def place(relative):
        return lax.rem(z + relative + NZ - NEAR, NZ)

    plane_row = place(iota((NZ, 1, 128), 0))
    numbers = [[], []]
    own_offset = jnp.sum(jnp.where(plane_row < z, by_plane, 0.0), axis=0)
    before = [own_offset]
    for group in range(2):
        relative = iota((NZ, 1, 128), 2) // HALF + group * (NZ // 2)
        offset = jnp.sum(jnp.where(plane_row < place(relative), by_plane, 0.0), axis=0)
        inside = lax.rem(iota((1, 128), 1), HALF).astype(F32)
        for part in range(NP):
            amount = jnp.sum(jnp.where(iota((NZ, 1, 128), 0) == relative, counts[part], 0.0), axis=0)
            for half in range(2):
                position = inside + float(half * HALF)
                numbers[half].append((part, group, jnp.where(position < amount, offset + position, -1.0)))
            offset = offset + amount
    for part in range(NP):
        own_offset = own_offset + jnp.where(part < p, counts[part, NEAR], 0.0)
    number = []
    for half in range(2):
        ordered = sorted(numbers[half], key=lambda item: item[:2])
        number.append(jnp.concatenate([value for _, _, value in ordered], axis=1))

    table = partner_ref[...].astype(F32)
    node = iota((1, NODES), 1).astype(F32)
    own_number = own_offset[:, :1] + iota((SLOTS, 1), 0).astype(F32)
    out_number = (iota((HALF, 1), 0) * NV + vol).astype(F32)
    wanted = jnp.concatenate([own_number, out_number], axis=0)
    mates = jnp.sum(jnp.where(node == wanted, table, 0.0), axis=1, keepdims=True)
    pick = jnp.concatenate([mates, out_number], axis=0)
    picked = [(number[half] == pick) for half in range(2)]
    ones = [jnp.where(match, 1.0, 0.0).astype(BF16) for match in picked]
    first = dot(jnp.concatenate([row_weight] + ones, axis=0), every)
    rows_term = first[:SLOTS, :E] + first[SLOTS:2 * SLOTS, E:]
    n_pick = SLOTS + 2 * HALF
    chosen = first[2 * SLOTS:2 * SLOTS + n_pick, :E] + first[2 * SLOTS + n_pick:, E:]
    companion = chosen[:SLOTS]

    arrived(tot_s.at[0:NP - 1], TOTAL)
    sums = [
        jnp.concatenate([tot_s[part, half:half + 1, :] for part in range(NP)], axis=1) for half in range(2)
    ]
    col_weight = jnp.concatenate(
        [exps[half * SLOTS:(half + 1) * SLOTS] * (1.0 / sums[half]) for half in range(2)], axis=0
    ).astype(BF16)
    second = dot(col_weight, every)
    cols_term = second[:SLOTS, :E] + second[SLOTS:, E:]

    d_embed = (rows_term + cols_term - 2.0 * companion) * (1.0 / TEMPERATURE)
    radial = jnp.sum(unit * d_embed, axis=1, keepdims=True)
    d_raw = jnp.where(live, inv_norm * (d_embed - unit * radial), 0.0).astype(BF16)
    g_proj = dot_tn(d_raw, pooled)
    d_sum = (dot(d_raw, proj_ref[...]) * (1.0 / PATCHES)).astype(BF16)
    d_sum32 = d_sum.astype(F32)
    g_out = dot(mix_turned, jnp.concatenate([d_sum] * 3, axis=0))
    d_mixed = twice(dot_nt(d_sum, w_out))
    d_spread = twice(d_sum32)

    def scatter(to):
        for dy, dx in apart:
            at = to * (NQ // 2) + ys[dy] * 4 + xs[dx]
            send(part_s.at[at], gath_s.at[piece], PIECE, (plane[dx] + to, ys[dy]))

        @pl.when(core != to)
        def _():
            at = to * (NQ // 2) + rep * 4 + x
            send(part_s.at[at], gath_s.at[piece], PIECE, (plane[0] + to, rep))

    for tile in range(NQ // 2):
        part_s[16 + tile, 0:8, :] = g_out[tile * 8:(tile + 1) * 8]
        part_s[16 + tile, 8:12, :] = g_proj[tile * 4:(tile + 1) * 4]
    scatter(1)

    g_mix = jnp.zeros((2 * C, 2 * C), F32)
    g_stem = jnp.zeros((2 * VOX, 2 * C), F32)
    for step in range(ROWS // CHUNK):
        rows = slice(step * CHUNK, (step + 1) * CHUNK)
        shape = (CHUNK // SLOTS, SLOTS, 2 * C)
        d_pre2 = (slope2_s[rows, :].reshape(shape) * d_mixed[None]).reshape(CHUNK, 2 * C).astype(BF16)
        g_mix = g_mix + dot(ht_s[:, rows], d_pre2)
        d_hid = (dot_nt(d_pre2, w_mix2).reshape(shape) + d_spread[None]).reshape(CHUNK, 2 * C)
        d_pre1 = (d_hid * slope1_s[rows, :]).astype(BF16)
        g_stem = g_stem + dot(xt_s[:, rows], d_pre1)
    g_mix = g_mix[:C, :C] + g_mix[C:, C:]
    g_stem = g_stem[:VOX, :C] + g_stem[VOX:, C:]
    for tile in range(NQ // 2):
        part_s[tile, 0:8, :] = g_mix[tile * 8:(tile + 1) * 8]
        part_s[tile, 8:12, :] = g_stem[tile * 4:(tile + 1) * 4]

    scatter(0)
    gath_s[piece] = part_s[piece]

    out_sum = jnp.zeros((HALF, 1), F32)
    for half in range(2):
        hit = picked[half][SLOTS + HALF:]
        out_sum = out_sum + jnp.sum(jnp.where(hit, sums[half], 0.0), axis=1, keepdims=True)
    affinity = jnp.sum(chosen[SLOTS:SLOTS + HALF] * chosen[SLOTS + HALF:], axis=1, keepdims=True)
    loss = jnp.log(out_sum) - affinity * (1.0 / TEMPERATURE)
    square = iota((HALF, HALF), 0) == iota((HALF, HALF), 1)
    loss_ref[...] = jnp.sum(jnp.where(square, loss, 0.0), axis=0, keepdims=True)

    arrived(gath_s.at[0:NQ - 1], PIECE)
    zed_s[z] = jnp.sum(gath_s[...], axis=0)
    for step in range(NZ // 2, 0, -1):
        for sign in (1, -1):
            if step < NZ // 2 or sign == 1:
                send(zed_s.at[z], zed_s.at[z], PIECE_Z, z_peer(sign * step))
    arrived(zed_s.at[0:NZ - 1], PIECE_Z)
    fin_s[piece] = jnp.sum(zed_s[...], axis=0)

    result = fin_s.at[piece]
    for dy, dx in apart:
        for to in range(2):
            send(result, result, RESULT, (plane[dx] + to, ys[dy]))
    send(result, result, RESULT, (plane[0] + mate, rep))
    arrived(fin_s.at[0:NQ - 1], RESULT)

    def normal(g):
        return g * lax.rsqrt(jnp.mean(g * g) + EPS)

    up_ref[0:64] = normal(jnp.concatenate([fin_s[tile, 8:12, :] for tile in range(16)], axis=0))
    up_ref[64:192] = normal(fin_s[0:16, 0:8, :].reshape(C, C))
    up_ref[192:320] = normal(fin_s[16:32, 0:8, :].reshape(C, C))
    up_ref[320:384] = normal(jnp.concatenate([fin_s[16 + tile, 8:12, :] for tile in range(16)], axis=0))

    for kind, ref in [
        (LINE_NEAR_A, emb_s.at[0, 0:4]), (LINE_NEAR_B, emb_s.at[0, 0:4]), (COUNT_NEAR, cnt_s.at[0, 0:8]),
        (LINE_FAR_A, emb_s.at[0, 0:4]), (LINE_FAR_B, emb_s.at[0, 0:3]), (COUNT_FAR, cnt_s.at[0, 0:7]),
        (PLANE_NEAR_A, emb_s.at[0:NP - 1, 0:5]), (PLANE_NEAR_B, emb_s.at[0:NP - 1, 0:4]),
        (PLANE_FAR_A, emb_s.at[0:NP - 1, 0:4]), (PLANE_FAR_B, emb_s.at[0:NP - 1, 0:3]),
        (PLANE_COUNT, cnt_s.at[0:NP - 1]), (TOTAL, tot_s.at[0:NP - 1]), (PIECE, gath_s.at[0:NQ - 1]),
        (PIECE_Z, zed_s.at[0:NZ - 1]), (RESULT, fin_s.at[0:NQ - 1]),
    ]:
        sent(ref, kind)


def store(up_ref, loss_ref, stem_hbm, mix_hbm, out_hbm, proj_hbm, loss_hbm, sem):
    copies = [
        pltpu.make_async_copy(source, target, sem.at[number])
        for number, (source, target) in enumerate([
            (up_ref.at[64:192], mix_hbm), (up_ref.at[192:320], out_hbm), (up_ref.at[0:64], stem_hbm),
            (up_ref.at[320:384], proj_hbm), (loss_ref, loss_hbm),
        ])
    ]
    for copy in copies:
        copy.start()
    for copy in copies:
        copy.wait()


def on_device(cutouts, counts, partner, w_stem, w_mix, w_out, w_proj):
    vmem = pl.BlockSpec(memory_space=pltpu.VMEM)
    hbm = pl.BlockSpec(memory_space=pltpu.HBM)
    updates, loss = pl.pallas_call(
        kernel,
        out_shape=(jax.ShapeDtypeStruct((384, 128), F32), jax.ShapeDtypeStruct((1, HALF), F32)),
        in_specs=[hbm] * 7,
        out_specs=(vmem,) * 2,
        scratch_shapes=[
            pltpu.VMEM((SLOTS, PATCHES * VOX), BF16),
            pltpu.VMEM((1, 1), jnp.int32),
            pltpu.VMEM((1, NODES), jnp.int32),
            pltpu.VMEM((VOX, C), BF16),
            pltpu.VMEM((C, C), BF16),
            pltpu.VMEM((C, C), BF16),
            pltpu.VMEM((E, C), BF16),
            pltpu.SemaphoreType.DMA((7,)),
            pltpu.VMEM((ROWS, 128), BF16),
            pltpu.VMEM((ROWS, 2 * C), BF16),
            pltpu.VMEM((ROWS, 2 * C), F32),
            pltpu.VMEM((ROWS, 2 * C), F32),
            pltpu.VMEM((128, ROWS), BF16),
            pltpu.VMEM((2 * C, ROWS), BF16),
            pltpu.VMEM((NP, NZ, HALF, 128), BF16),
            pltpu.VMEM((NP, NZ, 1, 128), F32),
            pltpu.VMEM((NP, 2, LINE), F32),
            pltpu.VMEM((NQ, 12, 128), F32),
            pltpu.VMEM((NQ, 12, 128), F32),
            pltpu.VMEM((NZ, 12, 128), F32),
            pltpu.VMEM((NQ, 12, 128), F32),
            pltpu.SemaphoreType.DMA((KINDS,)),
            pltpu.SemaphoreType.DMA((KINDS,)),
        ],
        compiler_params=pltpu.CompilerParams(
            collective_id=0, has_side_effects=True, vmem_limit_bytes=50000 * 1024
        ),
    )(*[v if v is counts else pltpu.with_memory_space_constraint(v, pltpu.HBM) for v in (cutouts[0], counts, partner, w_stem, w_mix, w_out, w_proj.T)])
    outs = pl.pallas_call(
        store,
        out_shape=(
            jax.ShapeDtypeStruct((VOX, C), F32),
            jax.ShapeDtypeStruct((C, C), F32),
            jax.ShapeDtypeStruct((C, C), F32),
            jax.ShapeDtypeStruct((E, C), F32),
            jax.ShapeDtypeStruct((1, HALF), F32),
        ),
        in_specs=[pl.BlockSpec(memory_space=pl.ANY)] * 2,
        out_specs=(hbm,) * 5,
        scratch_shapes=[pltpu.SemaphoreType.DMA((5,))],
        compiler_params=pltpu.CompilerParams(vmem_limit_bytes=4 * 1024 * 1024),
    )(updates, loss)
    return outs[:3] + (outs[3].T, outs[4][None])


def solution(mesh):
    in_specs = (P("rep", "vol", None), P("rep", "vol"), P("rep", None), P(), P(), P(), P())
    out_specs = (P(), P(), P(), P(), P("rep", "vol", None))
    return jax.shard_map(
        on_device, mesh=mesh, in_specs=in_specs, out_specs=out_specs, check_vma=False
    )
```

```python
import functools

import jax
import jax.numpy as jnp
from jax import lax
from jax.experimental import pallas as pl
from jax.experimental.pallas import tpu as pltpu
from jax.sharding import PartitionSpec as P

MESH = pl.DeviceIdType.MESH
F32 = jnp.float32
BF16 = jnp.bfloat16

NZ, NP, NY = 16, 8, 4
NV = NZ * NP
NQ = NP * NY
C, E, VOX, PATCHES = 128, 64, 64, 64
SLOTS, HALF = 32, 16
NODES = 2048
DEAD = NV * SLOTS - NODES
NEAR = 4
PAIRS = PATCHES // 2
ROWS = PAIRS * SLOTS
CHUNK = 256
LINE = NZ * HALF
TEMPERATURE = 0.2
LOG2E = 1.4426950408889634
SCALE = LOG2E / TEMPERATURE
EPS = 1e-6
(LINE_NEAR_A, LINE_NEAR_B, LINE_FAR_A, LINE_FAR_B, PLANE_NEAR_A, PLANE_NEAR_B, PLANE_FAR_A, PLANE_FAR_B,
 COUNT_NEAR, COUNT_FAR, PLANE_COUNT, TOTAL, PIECE, PIECE_Z, RESULT) = range(15)
KINDS = 15


def iota(shape, dim):
    return lax.broadcasted_iota(jnp.int32, shape, dim)


def dot(a, b):
    return lax.dot_general(a, b, (((1,), (0,)), ((), ())), preferred_element_type=F32)


def dot_nt(a, b):
    return lax.dot_general(a, b, (((1,), (1,)), ((), ())), preferred_element_type=F32)


def dot_tn(a, b):
    return lax.dot_general(a, b, (((0,), (0,)), ((), ())), preferred_element_type=F32)


def sigmoid(v):
    d = 1.0 + jnp.exp2(jnp.minimum(v * -LOG2E, 80.0 * LOG2E))
    r = pl.reciprocal(d, approx=True)
    return r * (2.0 - d * r)


def exact_terms(v):
    terms = []
    for _ in range(3):
        terms.append(v.astype(BF16))
        v = v - terms[-1].astype(F32)
    return jnp.concatenate(terms, axis=0)


def twice(v):
    return jnp.concatenate([v, v], axis=1)


def fold(v):
    half = v.shape[1] // 2
    return v[:, :half] + v[:, half:]


def block_diagonal(w):
    zero = jnp.zeros_like(w)
    return jnp.concatenate(
        [jnp.concatenate([w, zero], axis=1), jnp.concatenate([zero, w], axis=1)], axis=0
    )


def kernel(
    cut_hbm, count_hbm, partner_hbm, stem_hbm, mix_hbm, out_hbm, proj_hbm,
    up_ref, loss_ref,
    cut_ref, count_ref, partner_ref, stem_ref, mix_ref, out_ref, proj_ref, load_sem,
    x_s, hid_s, slope1_s, slope2_s, xt_s, ht_s,
    emb_s, cnt_s, tot_s, part_s, gath_s, zed_s, fin_s,
    send_sem, recv_sem,
):
    vol = lax.axis_index("vol")
    rep = lax.axis_index("rep")
    z = vol // NP
    p = lax.rem(vol, NP)
    x, core = p // 2, lax.rem(p, 2)
    xs = [lax.rem(x + step, 4) for step in range(4)]
    ys = [lax.rem(rep + step, 4) for step in range(4)]
    mate = 1 - core
    piece = core * (NQ // 2) + rep * 4 + x
    plane = [z * NP + xs[dx] * 2 for dx in range(4)]
    p_peers = [plane[dx] + to for dx in (2, 1, 3) for to in (core, mate)] + [plane[0] + mate]
    apart = sorted(
        [(dy, dx) for dy in range(4) for dx in range(4) if (dy, dx) != (0, 0)],
        key=lambda step: -min(step[0], 4 - step[0]) - min(step[1], 4 - step[1]),
    )

    def z_peer(step):
        return (lax.rem(z + step + NZ, NZ) * NP + p, rep)

    def send(src, dst, kind, device):
        pltpu.make_async_remote_copy(
            src_ref=src, dst_ref=dst, send_sem=send_sem.at[kind], recv_sem=recv_sem.at[kind],
            device_id=device, device_id_type=MESH,
        ).start()

    def arrived(ref, kind):
        pltpu.make_async_copy(ref, ref, recv_sem.at[kind]).wait()

    def sent(ref, kind):
        pltpu.make_async_copy(ref, ref, send_sem.at[kind]).wait()

    loads = [
        pltpu.make_async_copy(source, target, load_sem.at[number])
        for number, (source, target) in enumerate([
            (stem_hbm, stem_ref), (cut_hbm, cut_ref), (mix_hbm, mix_ref), (count_hbm, count_ref),
            (out_hbm, out_ref), (proj_hbm, proj_ref), (partner_hbm, partner_ref),
        ])
    ]
    for load in loads:
        load.start()

    barrier = pltpu.get_barrier_semaphore()
    greeted = 0
    for step in range(NEAR, 0, -1):
        for sign in (1, -1):
            pl.semaphore_signal(barrier, inc=1, device_id=z_peer(sign * step), device_id_type=MESH)
            greeted += 1
    for step in range(1, NY):
        pl.semaphore_signal(
            barrier, inc=1, device_id=(vol, ys[step]), device_id_type=MESH
        )
        greeted += 1
    for peer in p_peers:
        pl.semaphore_signal(barrier, inc=1, device_id=(peer, rep), device_id_type=MESH)
        greeted += 1

    loads[0].wait()
    w_stem2 = block_diagonal(stem_ref[...])
    loads[1].wait()
    loads[2].wait()
    w_mix2 = block_diagonal(mix_ref[...])
    hid_sum = mix_sum = jnp.zeros((SLOTS, 2 * C), F32)
    tall = (CHUNK // SLOTS, SLOTS, 2 * C)
    for first in range(0, ROWS, CHUNK):
        for pair in range(first // SLOTS, (first + CHUNK) // SLOTS):
            x_s[pair * SLOTS:(pair + 1) * SLOTS, :] = cut_ref[:, pair * 128:(pair + 1) * 128]
        rows = slice(first, first + CHUNK)
        pre1 = dot(x_s[rows, :], w_stem2)
        hidden = (pre1 * sigmoid(pre1)).astype(BF16)
        hid_s[rows, :] = hidden
        pre2 = dot(hidden, w_mix2)
        mixed = (pre2 * sigmoid(pre2)).astype(BF16)
        hid_sum = hid_sum + jnp.sum(hidden.astype(F32).reshape(tall), axis=0)
        mix_sum = mix_sum + jnp.sum(mixed.astype(F32).reshape(tall), axis=0)
    hid_sum, mix_sum = fold(hid_sum), fold(mix_sum)
    for load in loads[3:]:
        load.wait()
    count = count_ref[...]
    cnt_s[p, NEAR] = jnp.broadcast_to(count, (1, 128)).astype(F32)
    w_out = out_ref[...]
    mix_terms = exact_terms(mix_sum)
    branch = dot(mix_terms, w_out)
    branch = branch[:SLOTS] + branch[SLOTS:2 * SLOTS] + branch[2 * SLOTS:]
    pooled = ((hid_sum + branch) * (1.0 / PATCHES)).astype(BF16)
    raw = dot_nt(pooled, proj_ref[...])
    inv_norm = lax.rsqrt(jnp.sum(raw * raw, axis=1, keepdims=True) + EPS)
    unit = raw * inv_norm
    live = iota((SLOTS, E), 0) < count
    embed = jnp.where(live, unit, 0.0).astype(BF16)
    emb_s[p, NEAR] = jnp.concatenate([embed[:HALF], embed[HALF:]], axis=1)

    pl.semaphore_wait(barrier, greeted)

    own = emb_s.at[p, NEAR]
    own_count = cnt_s.at[p, NEAR]
    for step in range(NEAR, 0, -1):
        for sign in (1, -1):
            send(own, emb_s.at[p, NEAR - sign * step], LINE_NEAR_B if step > 2 else LINE_NEAR_A, z_peer(sign * step))
    for step in range(NEAR, 0, -1):
        for sign in (1, -1):
            send(own_count, cnt_s.at[p, NEAR - sign * step], COUNT_NEAR, z_peer(sign * step))

    def share(first, last, kind):
        block = emb_s.at[p, first:last]
        for peer in p_peers:
            send(block, block, kind, (peer, rep))

    def relay(source, target, blocks, kind, towards, ref=emb_s):
        send(ref.at[p, source:source + blocks], ref.at[p, target:target + blocks], kind, z_peer(towards))

    arrived(emb_s.at[0, 0:4], LINE_NEAR_A)
    relay(5, 9, 2, LINE_FAR_A, -NEAR)
    relay(2, 14, 2, LINE_FAR_A, NEAR)
    share(2, 7, PLANE_NEAR_A)
    arrived(emb_s.at[0, 0:4], LINE_NEAR_B)
    relay(7, 11, 2, LINE_FAR_B, -NEAR)
    relay(1, 13, 1, LINE_FAR_B, NEAR)
    share(0, 2, PLANE_NEAR_B)
    share(7, 9, PLANE_NEAR_B)
    arrived(cnt_s.at[0, 0:8], COUNT_NEAR)
    relay(5, 9, 4, COUNT_FAR, -NEAR, cnt_s)
    relay(1, 13, 3, COUNT_FAR, NEAR, cnt_s)

    def slopes(step, carry):
        rows = pl.ds(pl.multiple_of(step * CHUNK, CHUNK), CHUNK)
        pre1 = dot(x_s[rows, :], w_stem2)
        sig1 = sigmoid(pre1)
        slope1_s[rows, :] = sig1 * (1.0 + pre1 * (1.0 - sig1))
        pre2 = dot(hid_s[rows, :], w_mix2)
        sig2 = sigmoid(pre2)
        slope2_s[rows, :] = sig2 * (1.0 + pre2 * (1.0 - sig2))
        return carry

    lax.fori_loop(0, ROWS // CHUNK, slopes, 0)
    xt_s[...] = x_s[...].T
    ht_s[...] = hid_s[...].T
    mix_turned = mix_terms.T
    zero_slots = jnp.zeros((SLOTS, E), BF16)
    anchors = jnp.concatenate(
        [jnp.concatenate([embed, zero_slots], axis=1), jnp.concatenate([zero_slots, embed], axis=1)], axis=0
    )

    arrived(emb_s.at[0, 0:4], LINE_FAR_A)
    share(9, 11, PLANE_FAR_A)
    share(14, 16, PLANE_FAR_A)
    arrived(emb_s.at[0, 0:3], LINE_FAR_B)
    share(11, 14, PLANE_FAR_B)
    arrived(cnt_s.at[0, 0:7], COUNT_FAR)
    count_block = cnt_s.at[p]
    for peer in p_peers:
        send(count_block, count_block, PLANE_COUNT, (peer, rep))

    line = emb_s[p].reshape(LINE, 128)
    low = iota((LINE, 128), 1) < E
    turned = jnp.concatenate([line[:, E:], line[:, :E]], axis=1)
    none = jnp.zeros_like(line)
    columns = jnp.concatenate(
        [
            jnp.where(low, line, none), jnp.where(low, turned, none),
            jnp.where(low, none, turned), jnp.where(low, none, line),
        ],
        axis=0,
    )

    def powers(block, against):
        return jnp.exp2(dot_nt(block, against) * SCALE)

    def add_rows(total, first, last):
        block = emb_s[:, first:last].reshape(NP * (last - first) * HALF, 128)
        e = powers(block, columns)
        return total + jnp.sum(e.reshape(e.shape[0] // 8, 8, 4 * LINE), axis=0)

    diagonal = iota((LINE, LINE), 0) == iota((LINE, LINE), 1)
    self_sum = jnp.concatenate(
        [
            jnp.sum(jnp.where(diagonal, powers(line, columns[at:at + LINE]), 0.0), axis=0, keepdims=True)
            for at in (0, 3 * LINE)
        ],
        axis=1,
    )
    total = jnp.zeros((8, 4 * LINE), F32)
    arrived(emb_s.at[0:NP - 1, 0:5], PLANE_NEAR_A)
    total = add_rows(total, 2, 7)
    arrived(emb_s.at[0:NP - 1, 0:4], PLANE_NEAR_B)
    total = add_rows(add_rows(total, 0, 2), 7, 9)
    arrived(emb_s.at[0:NP - 1, 0:4], PLANE_FAR_A)
    total = add_rows(add_rows(total, 9, 11), 14, 16)
    arrived(emb_s.at[0:NP - 1, 0:3], PLANE_FAR_B)
    total = add_rows(total, 11, 14)
    line_sum = fold(jnp.sum(total, axis=0, keepdims=True)) - float(DEAD) - self_sum
    tot_s[p] = jnp.concatenate([line_sum[:, :LINE], line_sum[:, LINE:]], axis=0)
    own_total = tot_s.at[p]
    for peer in p_peers:
        send(own_total, own_total, TOTAL, (peer, rep))

    every = emb_s[...].reshape(NP * LINE, 128)
    wide = NP * LINE
    exps = jnp.exp2(dot_nt(anchors, every) * SCALE)
    row = iota((2 * SLOTS, wide), 0)
    col = iota((2 * SLOTS, wide), 1)
    slot = lax.rem(row, SLOTS)
    self_score = (row // SLOTS == slot // HALF) & (col == p * LINE + NEAR * HALF + lax.rem(slot, HALF))
    exps = jnp.where(self_score, 0.0, exps)
    row_sum = jnp.sum(exps, axis=1, keepdims=True)
    own_sum = row_sum[:SLOTS] + row_sum[SLOTS:] - float(DEAD)
    own_inv = 1.0 / own_sum
    row_weight = (exps * jnp.concatenate([own_inv, own_inv], axis=0)).astype(BF16)

    arrived(cnt_s.at[0:NP - 1], PLANE_COUNT)
    counts = cnt_s[...]
    by_plane = jnp.sum(counts, axis=0)

    def place(relative):
        return lax.rem(z + relative + NZ - NEAR, NZ)

    plane_row = place(iota((NZ, 1, 128), 0))
    numbers = [[], []]
    own_offset = jnp.sum(jnp.where(plane_row < z, by_plane, 0.0), axis=0)
    before = [own_offset]
    for group in range(2):
        relative = iota((NZ, 1, 128), 2) // HALF + group * (NZ // 2)
        offset = jnp.sum(jnp.where(plane_row < place(relative), by_plane, 0.0), axis=0)
        inside = lax.rem(iota((1, 128), 1), HALF).astype(F32)
        for part in range(NP):
            amount = jnp.sum(jnp.where(iota((NZ, 1, 128), 0) == relative, counts[part], 0.0), axis=0)
            for half in range(2):
                position = inside + float(half * HALF)
                numbers[half].append((part, group, jnp.where(position < amount, offset + position, -1.0)))
            offset = offset + amount
    for part in range(NP):
        own_offset = own_offset + jnp.where(part < p, counts[part, NEAR], 0.0)
    number = []
    for half in range(2):
        ordered = sorted(numbers[half], key=lambda item: item[:2])
        number.append(jnp.concatenate([value for _, _, value in ordered], axis=1))

    table = partner_ref[...].astype(F32)
    node = iota((1, NODES), 1).astype(F32)
    own_number = own_offset[:, :1] + iota((SLOTS, 1), 0).astype(F32)
    out_number = (iota((HALF, 1), 0) * NV + vol).astype(F32)
    wanted = jnp.concatenate([own_number, out_number], axis=0)
    mates = jnp.sum(jnp.where(node == wanted, table, 0.0), axis=1, keepdims=True)
    pick = jnp.concatenate([mates, out_number], axis=0)
    picked = [(number[half] == pick) for half in range(2)]
    ones = [jnp.where(match, 1.0, 0.0).astype(BF16) for match in picked]
    first = dot(jnp.concatenate([row_weight] + ones, axis=0), every)
    rows_term = first[:SLOTS, :E] + first[SLOTS:2 * SLOTS, E:]
    n_pick = SLOTS + 2 * HALF
    chosen = first[2 * SLOTS:2 * SLOTS + n_pick, :E] + first[2 * SLOTS + n_pick:, E:]
    companion = chosen[:SLOTS]

    arrived(tot_s.at[0:NP - 1], TOTAL)
    sums = [
        jnp.concatenate([tot_s[part, half:half + 1, :] for part in range(NP)], axis=1) for half in range(2)
    ]
    col_weight = jnp.concatenate(
        [exps[half * SLOTS:(half + 1) * SLOTS] * (1.0 / sums[half]) for half in range(2)], axis=0
    ).astype(BF16)
    second = dot(col_weight, every)
    cols_term = second[:SLOTS, :E] + second[SLOTS:, E:]

    d_embed = (rows_term + cols_term - 2.0 * companion) * (1.0 / TEMPERATURE)
    radial = jnp.sum(unit * d_embed, axis=1, keepdims=True)
    d_raw = jnp.where(live, inv_norm * (d_embed - unit * radial), 0.0).astype(BF16)
    g_proj = dot_tn(d_raw, pooled)
    d_sum = (dot(d_raw, proj_ref[...]) * (1.0 / PATCHES)).astype(BF16)
    d_sum32 = d_sum.astype(F32)
    g_out = dot(mix_turned, jnp.concatenate([d_sum] * 3, axis=0))
    d_mixed = twice(dot_nt(d_sum, w_out))
    d_spread = twice(d_sum32)

    def scatter(to, first, last):
        for dy, dx in apart:
            at = to * (NQ // 2) + ys[dy] * 4 + xs[dx]
            send(part_s.at[at, first:last], gath_s.at[piece, first:last], PIECE, (plane[dx] + to, ys[dy]))

        @pl.when(core != to)
        def _():
            at = to * (NQ // 2) + rep * 4 + x
            send(part_s.at[at, first:last], gath_s.at[piece, first:last], PIECE, (plane[0] + to, rep))

    for tile in range(NQ // 2):
        part_s[16 + tile, 0:8, :] = g_out[tile * 8:(tile + 1) * 8]
        part_s[16 + tile, 8:12, :] = g_proj[tile * 4:(tile + 1) * 4]
    scatter(1, 0, 12)

    g_mix = jnp.zeros((2 * C, 2 * C), F32)
    g_stem = jnp.zeros((2 * VOX, 2 * C), F32)
    shape = (CHUNK // SLOTS, SLOTS, 2 * C)
    d_pre2 = []
    for step in range(ROWS // CHUNK):
        rows = slice(step * CHUNK, (step + 1) * CHUNK)
        d_pre2.append((slope2_s[rows, :].reshape(shape) * d_mixed[None]).reshape(CHUNK, 2 * C).astype(BF16))
        g_mix = g_mix + dot(ht_s[:, rows], d_pre2[step])
    g_mix = g_mix[:C, :C] + g_mix[C:, C:]
    for tile in range(NQ // 2):
        part_s[tile, 0:8, :] = g_mix[tile * 8:(tile + 1) * 8]
    scatter(0, 0, 8)
    for step in range(ROWS // CHUNK):
        rows = slice(step * CHUNK, (step + 1) * CHUNK)
        d_hid = (dot_nt(d_pre2[step], w_mix2).reshape(shape) + d_spread[None]).reshape(CHUNK, 2 * C)
        d_pre1 = (d_hid * slope1_s[rows, :]).astype(BF16)
        g_stem = g_stem + dot(xt_s[:, rows], d_pre1)
    g_stem = g_stem[:VOX, :C] + g_stem[VOX:, C:]
    for tile in range(NQ // 2):
        part_s[tile, 8:12, :] = g_stem[tile * 4:(tile + 1) * 4]
    scatter(0, 8, 12)
    gath_s[piece] = part_s[piece]

    out_sum = jnp.zeros((HALF, 1), F32)
    for half in range(2):
        hit = picked[half][SLOTS + HALF:]
        out_sum = out_sum + jnp.sum(jnp.where(hit, sums[half], 0.0), axis=1, keepdims=True)
    affinity = jnp.sum(chosen[SLOTS:SLOTS + HALF] * chosen[SLOTS + HALF:], axis=1, keepdims=True)
    loss = jnp.log(out_sum) - affinity * (1.0 / TEMPERATURE)
    square = iota((HALF, HALF), 0) == iota((HALF, HALF), 1)
    loss_ref[...] = jnp.sum(jnp.where(square, loss, 0.0), axis=0, keepdims=True)

    arrived(gath_s.at[0:NQ - 1], PIECE)
    zed_s[z] = jnp.sum(gath_s[...], axis=0)
    for step in range(NZ // 2, 0, -1):
        for sign in (1, -1):
            if step < NZ // 2 or sign == 1:
                send(zed_s.at[z], zed_s.at[z], PIECE_Z, z_peer(sign * step))
    arrived(zed_s.at[0:NZ - 1], PIECE_Z)
    fin_s[piece] = jnp.sum(zed_s[...], axis=0)

    result = fin_s.at[piece]
    for dy, dx in apart:
        for to in range(2):
            send(result, result, RESULT, (plane[dx] + to, ys[dy]))
    send(result, result, RESULT, (plane[0] + mate, rep))
    arrived(fin_s.at[0:NQ - 1], RESULT)

    def normal(g):
        return g * lax.rsqrt(jnp.mean(g * g) + EPS)

    up_ref[0:64] = normal(jnp.concatenate([fin_s[tile, 8:12, :] for tile in range(16)], axis=0))
    up_ref[64:192] = normal(fin_s[0:16, 0:8, :].reshape(C, C))
    up_ref[192:320] = normal(fin_s[16:32, 0:8, :].reshape(C, C))
    up_ref[320:384] = normal(jnp.concatenate([fin_s[16 + tile, 8:12, :] for tile in range(16)], axis=0))

    for kind, ref in [
        (LINE_NEAR_A, emb_s.at[0, 0:4]), (LINE_NEAR_B, emb_s.at[0, 0:4]), (COUNT_NEAR, cnt_s.at[0, 0:8]),
        (LINE_FAR_A, emb_s.at[0, 0:4]), (LINE_FAR_B, emb_s.at[0, 0:3]), (COUNT_FAR, cnt_s.at[0, 0:7]),
        (PLANE_NEAR_A, emb_s.at[0:NP - 1, 0:5]), (PLANE_NEAR_B, emb_s.at[0:NP - 1, 0:4]),
        (PLANE_FAR_A, emb_s.at[0:NP - 1, 0:4]), (PLANE_FAR_B, emb_s.at[0:NP - 1, 0:3]),
        (PLANE_COUNT, cnt_s.at[0:NP - 1]), (TOTAL, tot_s.at[0:NP - 1]), (PIECE, gath_s.at[0:NQ - 1]),
        (PIECE_Z, zed_s.at[0:NZ - 1]), (RESULT, fin_s.at[0:NQ - 1]),
    ]:
        sent(ref, kind)


def store(up_ref, loss_ref, stem_hbm, mix_hbm, out_hbm, proj_hbm, loss_hbm, sem):
    copies = [
        pltpu.make_async_copy(source, target, sem.at[number])
        for number, (source, target) in enumerate([
            (up_ref.at[64:192], mix_hbm), (up_ref.at[192:320], out_hbm), (up_ref.at[0:64], stem_hbm),
            (up_ref.at[320:384], proj_hbm), (loss_ref, loss_hbm),
        ])
    ]
    for copy in copies:
        copy.start()
    for copy in copies:
        copy.wait()


def on_device(cutouts, counts, partner, w_stem, w_mix, w_out, w_proj):
    vmem = pl.BlockSpec(memory_space=pltpu.VMEM)
    hbm = pl.BlockSpec(memory_space=pltpu.HBM)
    updates, loss = pl.pallas_call(
        kernel,
        out_shape=(jax.ShapeDtypeStruct((384, 128), F32), jax.ShapeDtypeStruct((1, HALF), F32)),
        in_specs=[hbm] * 7,
        out_specs=(vmem,) * 2,
        scratch_shapes=[
            pltpu.VMEM((SLOTS, PATCHES * VOX), BF16),
            pltpu.VMEM((1, 1), jnp.int32),
            pltpu.VMEM((1, NODES), jnp.int32),
            pltpu.VMEM((VOX, C), BF16),
            pltpu.VMEM((C, C), BF16),
            pltpu.VMEM((C, C), BF16),
            pltpu.VMEM((E, C), BF16),
            pltpu.SemaphoreType.DMA((7,)),
            pltpu.VMEM((ROWS, 128), BF16),
            pltpu.VMEM((ROWS, 2 * C), BF16),
            pltpu.VMEM((ROWS, 2 * C), F32),
            pltpu.VMEM((ROWS, 2 * C), F32),
            pltpu.VMEM((128, ROWS), BF16),
            pltpu.VMEM((2 * C, ROWS), BF16),
            pltpu.VMEM((NP, NZ, HALF, 128), BF16),
            pltpu.VMEM((NP, NZ, 1, 128), F32),
            pltpu.VMEM((NP, 2, LINE), F32),
            pltpu.VMEM((NQ, 12, 128), F32),
            pltpu.VMEM((NQ, 12, 128), F32),
            pltpu.VMEM((NZ, 12, 128), F32),
            pltpu.VMEM((NQ, 12, 128), F32),
            pltpu.SemaphoreType.DMA((KINDS,)),
            pltpu.SemaphoreType.DMA((KINDS,)),
        ],
        compiler_params=pltpu.CompilerParams(
            collective_id=0, has_side_effects=True, vmem_limit_bytes=50000 * 1024
        ),
    )(*[v if v is counts else pltpu.with_memory_space_constraint(v, pltpu.HBM) for v in (cutouts[0], counts, partner, w_stem, w_mix, w_out, w_proj.T)])
    outs = pl.pallas_call(
        store,
        out_shape=(
            jax.ShapeDtypeStruct((VOX, C), F32),
            jax.ShapeDtypeStruct((C, C), F32),
            jax.ShapeDtypeStruct((C, C), F32),
            jax.ShapeDtypeStruct((E, C), F32),
            jax.ShapeDtypeStruct((1, HALF), F32),
        ),
        in_specs=[pl.BlockSpec(memory_space=pl.ANY)] * 2,
        out_specs=(hbm,) * 5,
        scratch_shapes=[pltpu.SemaphoreType.DMA((5,))],
        compiler_params=pltpu.CompilerParams(vmem_limit_bytes=4 * 1024 * 1024),
    )(updates, loss)
    return outs[:3] + (outs[3].T, outs[4][None])


def solution(mesh):
    in_specs = (P("rep", "vol", None), P("rep", "vol"), P("rep", None), P(), P(), P(), P())
    out_specs = (P(), P(), P(), P(), P("rep", "vol", None))
    return jax.shard_map(
        on_device, mesh=mesh, in_specs=in_specs, out_specs=out_specs, check_vma=False
    )
```
